256 devices in a mesh: gx: 32 (over z_hi, x, y), gy: 8 (over z_lo, core).
Axes of the slice: x: 4, y: 4, z: 8 (z_hi: 2, z_lo: 4; z = z_hi * 4 + z_lo), core: 2. Of those that a mesh axis runs over, the one named last changes fastest.
Arguments:
- bead_charge: float32 [32, 8, 16384], P('gx', 'gy'), may hold values from -6 to 6
- bead_cell: int32 [32, 8, 16384], P('gx', 'gy'), may hold values from 0 to 32767
- bead_count: int32 [32, 8], P('gx', 'gy'), may hold values from 8192 to 16384
- interp_weights: bfloat16 [32, 8, 12, 16384], P('gx', 'gy'), may hold values from 0.049804688 to 0.59765625
- kernel_fine: bfloat16 [17, 17, 17], replicated, may hold values from 0 to 4
- kernel_coarse: bfloat16 [17, 17, 17], replicated, may hold values from 0 to 4
Outputs:
- bead_potential: float32 [32, 8, 16384], P('gx', 'gy')
- potential_grid: float32 [512, 128, 128], P('gx', 'gy')
The draws below stay inside these ranges and needn't reach their ends.
All inputs are finite; a program needn't handle non-finite values.
Results may differ from the reference program's by a relative error of at most 0.00076.
Values may be sent and summed in bfloat16 or wider, within the bound.
A program may use at most 64 MiB of HBM per device.

```python
import jax
import jax.numpy as jnp

LX = 16
LY = 16
LZ = 128
SLOTS = 16384
RADIUS = 8
NX = 512
NY = 128
NZ = 128
N_GX = 32
N_GY = 8


def kernel_shape(key, spread):
    side = 2 * RADIUS + 1
    offsets = jnp.arange(side, dtype=jnp.float32) - float(RADIUS)
    squared = offsets[:, None, None] * offsets[:, None, None] + offsets[None, :, None] * offsets[None, :, None] + offsets[None, None, :] * offsets[None, None, :]
    radius_cells = jnp.sqrt(squared)
    envelope = 1.0 / (1.0 + radius_cells / 6.0)
    jitter = jax.random.uniform(key, (side, side, side), jnp.float32, 1.0 - spread, 1.0 + spread)
    values = envelope * jitter
    return values * (4.0 / jnp.sqrt(jnp.sum(values * values)))


def draw_kernel_fine(key, part):
    values = kernel_shape(jax.random.fold_in(key, 11), 0.5)
    return values.astype(jnp.bfloat16)


def draw_kernel_coarse(key, part):
    values = kernel_shape(jax.random.fold_in(key, 23), 0.5)
    return values.astype(jnp.bfloat16)


def set_ends(array, stream_key, least, top_value):
    index_at = [jax.random.randint(jax.random.fold_in(stream_key, axis), (), 0, length) for axis, length in enumerate(array.shape)]
    main_axis = array.shape.index(max(array.shape))
    next_to = index_at[:main_axis] + [(index_at[main_axis] + 1) % array.shape[main_axis]] + index_at[main_axis + 1:]
    return array.at[tuple(index_at)].set(least).at[tuple(next_to)].set(top_value)


def steps_of(key, extent, split, smallest, high):
    gain, own = 1.0, jax.random.fold_in(key, 6)
    for axis_at, parts in split:
        heights = jnp.exp(jax.random.uniform(jax.random.fold_in(own, axis_at), (parts,), jnp.float32, smallest / len(split), high / len(split)))
        gain = gain * jnp.repeat(heights, extent[axis_at] // parts).reshape([-1 if axis == axis_at else 1 for axis in range(len(extent))])
    return gain


def gaussian(stream_key, dims, scale, bound, shards=(), kind=jnp.bfloat16):
    result = jax.random.normal(stream_key, dims, jnp.float32) * scale
    if len(shards) > 0:
        result = steps_of(stream_key, dims, shards, -0.22, 0.18) * result
    return jnp.clip(result, min=-bound, max=bound).astype(kind)


def setup_inputs(seed: int = 0) -> dict:
    key_list = jax.random.split(jax.random.key(seed), 7)
    return {
        "bead_charge": gaussian(key_list[0], (N_GX, N_GY, SLOTS), 1.0, 6.0, ((0, 32), (1, 8)), jnp.float32),
        "bead_cell": set_ends(jax.random.randint(key_list[1], (N_GX, N_GY, SLOTS), 0, LX * LY * LZ), jax.random.fold_in(key_list[1], 1), 0, (LX * LY * LZ) - 1).astype(jnp.int32),
        "bead_count": set_ends(jax.random.randint(key_list[2], (N_GX, N_GY), SLOTS // 2, SLOTS + 1), jax.random.fold_in(key_list[2], 1), SLOTS // 2, SLOTS).astype(jnp.int32),
        "interp_weights": jnp.clip(0.049804688 + 0.54785156 * jax.random.uniform(key_list[3], (N_GX, N_GY, 12, SLOTS), jnp.float32) ** steps_of(key_list[3], (N_GX, N_GY, 12, SLOTS), ((0, 32), (1, 8)), -0.2, 0.2), 0.049804688, 0.59765625).astype(jnp.bfloat16),
        "kernel_fine": draw_kernel_fine(jax.random.fold_in(key_list[6], 71), 0),
        "kernel_coarse": draw_kernel_coarse(jax.random.fold_in(key_list[6], 71), 0),
    }


SPLINE = (0.125, 0.5, 0.75, 0.5, 0.125)


def correlate(grid, kernel):
    shape_grid = grid.shape
    radius = (kernel.shape[0] - 1) // 2
    taps = jnp.arange(kernel.shape[0], dtype=jnp.int32) - radius
    index_first = ((-taps) % shape_grid[0])[:, None, None]
    index_second = ((-taps) % shape_grid[1])[None, :, None]
    index_third = ((-taps) % shape_grid[2])[None, None, :]
    table = jnp.zeros(shape_grid, grid.dtype)
    table = table.at[index_first, index_second, index_third].add(kernel.astype(grid.dtype))
    spectrum = jnp.fft.rfftn(grid) * jnp.fft.rfftn(table)
    return jnp.fft.irfftn(spectrum, s=shape_grid).astype(grid.dtype)


def restrict_grid(grid):
    for axis_number in range(3):
        summed = SPLINE[0] * jnp.roll(grid, 2, axis_number)
        for offset_one in range(1, 5):
            summed = summed + SPLINE[offset_one] * jnp.roll(grid, 2 - offset_one, axis_number)
        moved = jnp.moveaxis(summed, axis_number, 0)[::2]
        grid = jnp.moveaxis(moved, 0, axis_number)
    return grid


def refine_grid(grid):
    for axis_number in range(3):
        middle = jnp.moveaxis(grid, axis_number, 0)
        lower = jnp.roll(middle, 1, 0)
        upper = jnp.roll(middle, -1, 0)
        even_rows = (lower + 6.0 * middle + upper) * 0.125
        odd_rows = (middle + upper) * 0.5
        joined = jnp.stack([even_rows, odd_rows], axis=1).reshape((2 * middle.shape[0],) + middle.shape[1:])
        grid = jnp.moveaxis(joined, 0, axis_number)
    return grid


def reference(bead_charge, bead_cell, bead_count, interp_weights, kernel_fine, kernel_coarse):
    slot_index = jnp.arange(SLOTS, dtype=jnp.int32)
    live_slots = slot_index[None, None, :] < bead_count[:, :, None]
    values = jnp.where(live_slots, bead_charge, jnp.zeros_like(bead_charge))
    weights = interp_weights.astype(jnp.float32)
    brick_first = jnp.arange(N_GX, dtype=jnp.int32)[:, None, None]
    brick_second = jnp.arange(N_GY, dtype=jnp.int32)[None, :, None]
    cell_first = bead_cell // (LY * LZ) + brick_first * LX
    cell_second = (bead_cell // LZ) % LY + brick_second * LY
    cell_third = bead_cell % LZ
    charges = jnp.zeros((NX, NY, NZ), jnp.float32)
    for offset_one in range(4):
        for offset_two in range(4):
            for offset_three in range(4):
                contribution = values * weights[:, :, offset_one] * weights[:, :, 4 + offset_two] * weights[:, :, 8 + offset_three]
                charges = charges.at[(cell_first + offset_one) % NX, (cell_second + offset_two) % NY, (cell_third + offset_three) % NZ].add(contribution)
    fine_grid = charges.astype(jnp.bfloat16)
    fine_values = fine_grid.astype(jnp.float32)
    coarse_grid = restrict_grid(fine_values).astype(jnp.bfloat16)
    coarse_potential = correlate(coarse_grid.astype(jnp.float32), kernel_coarse.astype(jnp.float32))
    potential_grid = correlate(fine_values, kernel_fine.astype(jnp.float32)) + refine_grid(coarse_potential)
    bead_sum = jnp.zeros(values.shape, jnp.float32)
    for offset_one in range(4):
        for offset_two in range(4):
            for offset_three in range(4):
                factor = weights[:, :, offset_one] * weights[:, :, 4 + offset_two] * weights[:, :, 8 + offset_three]
                picked = potential_grid[(cell_first + offset_one) % NX, (cell_second + offset_two) % NY, (cell_third + offset_three) % NZ]
                bead_sum = bead_sum + factor * picked
    bead_potential = jnp.where(live_slots, bead_sum, jnp.zeros_like(bead_sum))
    return bead_potential, potential_grid
```

```python
import functools

import jax
import jax.numpy as jnp
from jax import lax
from jax.experimental import pallas as pl
from jax.experimental.pallas import tpu as pltpu
from jax.sharding import PartitionSpec as P

LX = 16
LY = 16
LZ = 128
SIDE = 17
BLOCK = 1024
ROWS = 384
MESH = pl.DeviceIdType.MESH
F32 = jnp.float32
BF16 = jnp.bfloat16
LANES_BOTH = (((1,), (1,)), ((), ()))


def iota(shape, dim):
    return lax.broadcasted_iota(jnp.int32, shape, dim)


def split(value):
    high = value.astype(BF16)
    low = (value - high.astype(F32)).astype(BF16)
    return high, low


def bead_tables(cells, weights, scale):
    count = cells.shape[1]
    first = cells >> 11
    second = (cells >> 7) & 15
    third = cells & 127
    rows = iota((24, count), 0)
    away_first = rows - first
    away_second = rows - second
    rows_first = jnp.zeros((24, count), F32)
    rows_second = jnp.zeros((24, count), F32)
    for tap in range(4):
        amount = weights[tap : tap + 1]
        if scale is not None:
            amount = amount * scale
        rows_first = jnp.where(away_first == tap, amount, rows_first)
        rows_second = jnp.where(away_second == tap, weights[4 + tap : 5 + tap], rows_second)
    depth = jnp.zeros((LZ, count), F32)
    away = (iota((LZ, count), 0) - third) & 127
    for tap in range(4):
        depth = jnp.where(away == tap, weights[8 + tap : 9 + tap], depth)
    return rows_first, rows_second, depth.astype(BF16)


def spread_kernel(count_ref, charge_ref, cell_ref, weight_ref, main_ref, tail_ref, total):
    live = count_ref[0, 0]
    total[...] = jnp.zeros_like(total)

    def add_block(step, carry):
        start = pl.multiple_of(step * BLOCK, BLOCK)
        here = pl.ds(start, BLOCK)
        slots = iota((1, BLOCK), 1) + start
        charge = jnp.where(slots < live, charge_ref[:, here], 0.0)
        weights = weight_ref[:, here].astype(F32)
        rows_first, rows_second, depth = bead_tables(cell_ref[:, here], weights, charge)
        parts = [rows_first[x : x + 1] * rows_second[:16] for x in range(19)]
        parts += [rows_second[y : y + 1] * rows_first for y in range(16, 19)]
        parts += [jnp.zeros((8, BLOCK), F32)]
        high, low = split(jnp.concatenate(parts, axis=0))
        total[...] += lax.dot_general(
            high, depth, LANES_BOTH, preferred_element_type=F32
        ) + lax.dot_general(low, depth, LANES_BOTH, preferred_element_type=F32)
        return carry

    lax.fori_loop(0, charge_ref.shape[1] // BLOCK, add_block, 0)
    main_ref[...] = total[0:304].reshape(19, 16, LZ)
    tail_ref[...] = total[304:376].reshape(3, 24, LZ)


def read_kernel(count_ref, cell_ref, weight_ref, main_ref, tail_ref, bead_ref, grid_ref, table):
    live = count_ref[0, 0]
    grid_ref[...] = main_ref[0:16]
    flat = jnp.concatenate(
        [main_ref[...].reshape(304, LZ), tail_ref[...].reshape(72, LZ), jnp.zeros((8, LZ), F32)],
        axis=0,
    )
    high, low = split(flat)
    table[:, 0:LZ] = high
    table[:, LZ:] = low

    def read_block(step, carry):
        start = pl.multiple_of(step * BLOCK, BLOCK)
        here = pl.ds(start, BLOCK)
        weights = weight_ref[:, here].astype(F32)
        rows_first, rows_second, depth = bead_tables(cell_ref[:, here], weights, None)
        along = jnp.dot(
            table[...], jnp.concatenate([depth, depth], axis=0), preferred_element_type=F32
        )
        near = jnp.zeros((16, BLOCK), F32)
        for x in range(19):
            near = near + rows_first[x : x + 1] * along[16 * x : 16 * x + 16]
        far = jnp.zeros((24, BLOCK), F32)
        for y in range(3):
            far = far + rows_second[16 + y : 17 + y] * along[304 + 24 * y : 328 + 24 * y]
        near = near * rows_second[:16]
        far = far * rows_first
        both = near[:8] + near[8:] + far[:8] + far[8:16] + far[16:]
        slots = iota((1, BLOCK), 1) + start
        value = jnp.sum(both, axis=0, keepdims=True)
        bead_ref[:, here] = jnp.where(slots < live, value, 0.0)
        return carry

    lax.fori_loop(0, cell_ref.shape[1] // BLOCK, read_block, 0)


AROUND = [(a, b) for a in (-1, 0, 1) for b in (-1, 0, 1) if (a, b) != (0, 0)]


def middle_kernel(
    sizes,
    main_ref,
    tail_ref,
    fine_ref,
    coarse_ref,
    pmain_ref,
    ptail_ref,
    side_first,
    side_second,
    side_both,
    charges,
    out_edge,
    out_corner,
    in_edge,
    in_corner,
    grid,
    shifted,
    summed,
    lines,
    fine_table,
    coarse_table,
    own_coarse,
    in_coarse,
    wide_coarse,
    shifted_coarse,
    total,
    own_pot,
    in_pot,
    wide_pot,
    rows_pot,
    send_tail,
    potential,
    send_1,
    recv_1,
    send_2,
    recv_2,
    send_3,
    recv_3,
    send_4,
    recv_4,
    send_5,
    recv_5,
):
    here_first = lax.axis_index("gx")
    here_second = lax.axis_index("gy")

    def device(a, b):
        return (
            lax.rem(here_first + (a + sizes[0]), sizes[0]),
            lax.rem(here_second + (b + sizes[1]), sizes[1]),
        )

    def send(source, target, out_sem, in_sem, a, b):
        copy = pltpu.make_async_remote_copy(
            src_ref=source,
            dst_ref=target,
            send_sem=out_sem,
            recv_sem=in_sem,
            device_id=device(a, b),
            device_id_type=MESH,
        )
        copy.start()
        return copy

    barrier = pltpu.get_barrier_semaphore()
    for a, b in AROUND:
        pl.semaphore_signal(barrier, inc=1, device_id=device(a, b), device_id_type=MESH)
    pl.semaphore_wait(barrier, 8)

    spills = [
        send(main_ref.at[16:19], side_first, send_1.at[0], recv_1.at[0], 1, 0),
        send(tail_ref.at[:, 0:16], side_second, send_1.at[1], recv_1.at[1], 0, 1),
        send(tail_ref.at[:, 16:24], side_both, send_1.at[2], recv_1.at[2], 1, 1),
    ]

    taps = iota((SIDE, LZ), 0)
    lanes = iota((SIDE, LZ), 1)
    place_fine = (((lanes + taps - 8) & 127) == 0).astype(BF16)
    place_coarse = (((lanes + taps - 8) & 63) == 0).astype(BF16)
    lines[18, 0:SIDE] = jnp.zeros((SIDE, LZ), F32)
    lines[36, 0:SIDE] = jnp.zeros((SIDE, LZ), F32)
    for dx in range(SIDE):
        lines[dx, 0:SIDE] = jnp.dot(fine_ref[dx], place_fine, preferred_element_type=F32)
        lines[19 + dx, 0:SIDE] = jnp.dot(coarse_ref[dx], place_coarse, preferred_element_type=F32)

    def first_rows(line):
        return pltpu.roll(
            jnp.broadcast_to(line, (8, LZ)), 0, 1, stride=1, stride_axis=0
        )

    def turned(base, shift):
        return base if shift == 0 else pltpu.roll(base, shift, 1)

    def build_fine(dx, carry):
        for dy in range(SIDE):
            base = first_rows(lines[dx, dy : dy + 1])
            rows = [turned(base, 8 * i) for i in range(16)]
            fine_table[dx, 128 * dy : 128 * dy + 128] = jnp.concatenate(rows, axis=0).astype(BF16)
        return carry

    lax.fori_loop(0, SIDE, build_fine, 0)

    for copy in spills:
        copy.wait()
    charges[...] = main_ref[0:16]
    charges[0:3] += side_first[...]
    for y in range(3):
        side_second[y, 0:8] += side_both[y]
        charges[:, y, :] += side_second[y]
    rounded = charges[...].astype(BF16).astype(F32)
    grid[8:24, 8:24] = rounded

    halves = [grid[8:24, 8:16], grid[8:24, 16:24]]
    out_edge[0] = grid[8:16, 8:24].astype(BF16)
    out_edge[1] = grid[16:24, 8:24].astype(BF16)
    out_edge[2] = halves[0].reshape(8, 16, LZ).astype(BF16)
    out_edge[3] = halves[1].reshape(8, 16, LZ).astype(BF16)
    for i in range(2):
        for j in range(2):
            quarter = grid[8 + 8 * i : 16 + 8 * i, 8 + 8 * j : 16 + 8 * j]
            out_corner[2 * i + j] = quarter.reshape(4, 16, LZ).astype(BF16)
    halos = []
    for at, (a, b) in enumerate([(-1, 0), (1, 0), (0, -1), (0, 1)]):
        halos.append(send(out_edge.at[at], in_edge.at[at], send_2.at[at], recv_2.at[at], a, b))
    for at, (a, b) in enumerate([(-1, -1), (-1, 1), (1, -1), (1, 1)]):
        halos.append(
            send(out_corner.at[at], in_corner.at[at], send_2.at[4 + at], recv_2.at[4 + at], a, b)
        )

    lower_half = iota((64, LZ), 1) < 64

    def build_coarse(m, carry):
        for dy in range(SIDE):
            blocks = []
            for step in range(3):
                base = first_rows(lines[18 + 2 * m + step, dy : dy + 1])
                blocks.append(jnp.concatenate([turned(base, 8 * i) for i in range(8)], axis=0))
            pair = [
                jnp.where(lower_half, blocks[1], blocks[0]),
                jnp.where(lower_half, blocks[2], blocks[1]),
            ]
            coarse_table[m, 128 * dy : 128 * dy + 128] = jnp.concatenate(pair, axis=0).astype(BF16)
        return carry

    lax.fori_loop(0, 9, build_coarse, 0)

    for copy in halos:
        copy.wait()
    grid[24:32, 8:24] = in_edge[0].astype(F32)
    grid[0:8, 8:24] = in_edge[1].astype(F32)
    grid[8:24, 24:32] = in_edge[2].astype(F32).reshape(16, 8, LZ)
    grid[8:24, 0:8] = in_edge[3].astype(F32).reshape(16, 8, LZ)
    for i in range(2):
        for j in range(2):
            quarter = in_corner[2 * i + j].astype(F32).reshape(8, 8, LZ)
            grid[24 - 24 * i : 32 - 24 * i, 24 - 24 * j : 32 - 24 * j] = quarter

    gap = (iota((LZ, LZ), 0) - 2 * (iota((LZ, LZ), 1) & 63) + 2) & 127
    spline = jnp.where(gap == 2, 0.75, 0.0)
    spline = jnp.where((gap == 1) | (gap == 3), 0.5, spline)
    spline = jnp.where((gap == 0) | (gap == 4), 0.125, spline).astype(BF16)
    coarse_lines = jnp.dot(
        grid[6:25].reshape(19 * 32, LZ).astype(BF16), spline, preferred_element_type=F32
    ).reshape(19, 32, LZ)
    for i in range(8):
        summed[i] = (
            0.125 * (coarse_lines[2 * i] + coarse_lines[2 * i + 4])
            + 0.5 * (coarse_lines[2 * i + 1] + coarse_lines[2 * i + 3])
            + 0.75 * coarse_lines[2 * i + 2]
        )
    lower_8 = iota((8, LZ), 1) < 64
    for j in range(4):
        planes = []
        for i in (2 * j, 2 * j + 1):
            parts = [summed[i, pl.ds(6 + t, 8, stride=2)] for t in range(5)]
            planes.append(
                0.125 * (parts[0] + parts[4]) + 0.5 * (parts[1] + parts[3]) + 0.75 * parts[2]
            )
        own_coarse[j] = jnp.where(lower_8, planes[0], planes[1]).astype(BF16).astype(F32)
    coarse_sends = []
    for at, (a, b) in enumerate(AROUND):
        coarse_sends.append(send(own_coarse, in_coarse.at[at], send_3.at[at], recv_3.at[at], a, b))

    for dy in range(SIDE):
        shifted[dy] = grid[:, dy : dy + 16].astype(BF16)
    total[...] = jnp.zeros_like(total)

    def correlate_fine(dx, carry):
        acc = total[...]
        for dy in range(0, SIDE, 2):
            depth = min(2, SIDE - dy)
            left = [shifted[dy + k, pl.ds(dx, 16)].reshape(256, LZ) for k in range(depth)]
            acc = acc + jnp.dot(
                jnp.concatenate(left, axis=1),
                fine_table[dx, 128 * dy : 128 * (dy + depth)],
                preferred_element_type=F32,
            )
        total[...] = acc
        return carry

    lax.fori_loop(0, 9, correlate_fine, 0)

    for copy in coarse_sends:
        copy.wait()
    wide_coarse[4:8, 8:16] = own_coarse[...]
    for at, (a, b) in enumerate(AROUND):
        wide_coarse[4 - 4 * a : 8 - 4 * a, 8 - 8 * b : 16 - 8 * b] = in_coarse[at]
    for dy in range(SIDE):
        shifted_coarse[dy] = wide_coarse[:, dy : dy + 8]

    def correlate_coarse(m, acc):
        for dy in range(0, SIDE, 2):
            depth = min(2, SIDE - dy)
            left = [
                shifted_coarse[dy + k, pl.ds(m, 4)].reshape(32, LZ).astype(BF16)
                for k in range(depth)
            ]
            acc = acc + jnp.dot(
                jnp.concatenate(left, axis=1),
                coarse_table[m, 128 * dy : 128 * (dy + depth)],
                preferred_element_type=F32,
            )
        return acc

    own_pot[...] = lax.fori_loop(0, 9, correlate_coarse, jnp.zeros((32, LZ), F32)).reshape(
        4, 8, LZ
    )
    pot_sends = []
    for at, (a, b) in enumerate(AROUND):
        span = slice(0, 4) if a == 0 else (slice(0, 1) if a < 0 else slice(3, 4))
        land = slice(0, 4) if a == 0 else slice(0, 1)
        pot_sends.append(
            send(own_pot.at[span], in_pot.at[at, land], send_4.at[at], recv_4.at[at], a, b)
        )

    lax.fori_loop(9, SIDE, correlate_fine, 0)

    for copy in pot_sends:
        copy.wait()
    wide_pot[1:5, 8:16] = own_pot[...]
    for at, (a, b) in enumerate(AROUND):
        first = slice(1, 5) if a == 0 else (slice(5, 6) if a < 0 else slice(0, 1))
        land = slice(0, 4) if a == 0 else slice(0, 1)
        wide_pot[first, 8 - 8 * b : 16 - 8 * b] = in_pot[at, land]
    planes = [pltpu.roll(wide_pot[0], 64, 1)]
    for j in range(1, 5):
        planes += [wide_pot[j], pltpu.roll(wide_pot[j], 64, 1)]
    planes += [wide_pot[5]]
    for i in range(8):
        rows_pot[2 * i] = (planes[i] + 6.0 * planes[i + 1] + planes[i + 2]) * 0.125
        rows_pot[2 * i + 1] = (planes[i + 1] + planes[i + 2]) * 0.5
    below = rows_pot[:, 7:15]
    middle = rows_pot[:, 8:16]
    above = rows_pot[:, 9:17]
    even_rows = (below + 6.0 * middle + above) * 0.125
    odd_rows = (middle + above) * 0.5
    for i in range(16):
        potential[i, pl.ds(0, 8, stride=2)] = even_rows[i]
        potential[i, pl.ds(1, 8, stride=2)] = odd_rows[i]
    source = iota((LZ, LZ), 0)
    offset = (iota((LZ, LZ), 1) - 2 * source + 1) & 127
    refine = jnp.where((offset == 0) | (offset == 2), 0.5, 0.0)
    refine = jnp.where(offset == 1, 0.75, refine)
    far = (iota((LZ, LZ), 1) - 2 * source + 2) & 127
    refine = jnp.where((far == 0) | (far == 4), 0.125, refine)
    refine = jnp.where(source < 64, refine, 0.0).astype(BF16)
    high, low = split(potential[...].reshape(256, LZ))
    smooth = jnp.dot(
        jnp.concatenate([high, low], axis=1),
        jnp.concatenate([refine, refine], axis=0),
        preferred_element_type=F32,
    )
    potential[...] = (total[...] + smooth).reshape(16, 16, LZ)

    for y in range(3):
        send_tail[y] = potential[:, y, :]
    upper = [
        send(potential.at[0:3], pmain_ref.at[16:19], send_5.at[0], recv_5.at[0], -1, 0),
        send(send_tail, ptail_ref.at[:, 0:16], send_5.at[1], recv_5.at[1], 0, -1),
        send(send_tail.at[:, 0:8], ptail_ref.at[:, 16:24], send_5.at[2], recv_5.at[2], -1, -1),
    ]
    pmain_ref[0:16] = potential[...]
    for copy in upper:
        copy.wait()


def on_device(sizes, bead_charge, bead_cell, bead_count, interp_weights, kernel_fine, kernel_coarse):
    slots = bead_charge.shape[-1]
    charge = bead_charge.reshape(1, slots)
    cells = bead_cell.reshape(1, slots)
    weights = interp_weights.reshape(12, slots)
    vmem = pl.BlockSpec(memory_space=pltpu.VMEM)
    smem = pl.BlockSpec(memory_space=pltpu.SMEM)
    main, tail = pl.pallas_call(
        spread_kernel,
        out_shape=(
            jax.ShapeDtypeStruct((19, 16, LZ), F32),
            jax.ShapeDtypeStruct((3, 24, LZ), F32),
        ),
        in_specs=[smem, vmem, vmem, vmem],
        out_specs=(vmem, vmem),
        scratch_shapes=[pltpu.VMEM((ROWS, LZ), F32)],
        compiler_params=pltpu.CompilerParams(vmem_limit_bytes=40 << 20),
        name="spread",
    )(bead_count, charge, cells, weights)
    dma = pltpu.SemaphoreType.DMA
    pmain, ptail = pl.pallas_call(
        functools.partial(middle_kernel, sizes),
        out_shape=(
            jax.ShapeDtypeStruct((19, 16, LZ), F32),
            jax.ShapeDtypeStruct((3, 24, LZ), F32),
        ),
        in_specs=[vmem] * 4,
        out_specs=(vmem, vmem),
        scratch_shapes=[
            pltpu.VMEM((3, 16, LZ), F32),
            pltpu.VMEM((3, 16, LZ), F32),
            pltpu.VMEM((3, 8, LZ), F32),
            pltpu.VMEM((16, 16, LZ), F32),
            pltpu.VMEM((4, 8, 16, LZ), BF16),
            pltpu.VMEM((4, 4, 16, LZ), BF16),
            pltpu.VMEM((4, 8, 16, LZ), BF16),
            pltpu.VMEM((4, 4, 16, LZ), BF16),
            pltpu.VMEM((32, 32, LZ), F32),
            pltpu.VMEM((SIDE, 32, 16, LZ), BF16),
            pltpu.VMEM((8, 32, LZ), F32),
            pltpu.VMEM((37, 24, LZ), F32),
            pltpu.VMEM((SIDE, SIDE * LZ, LZ), BF16),
            pltpu.VMEM((9, SIDE * LZ, LZ), BF16),
            pltpu.VMEM((4, 8, LZ), F32),
            pltpu.VMEM((8, 4, 8, LZ), F32),
            pltpu.VMEM((12, 24, LZ), F32),
            pltpu.VMEM((SIDE, 12, 8, LZ), F32),
            pltpu.VMEM((256, LZ), F32),
            pltpu.VMEM((4, 8, LZ), F32),
            pltpu.VMEM((8, 4, 8, LZ), F32),
            pltpu.VMEM((6, 24, LZ), F32),
            pltpu.VMEM((16, 24, LZ), F32),
            pltpu.VMEM((3, 16, LZ), F32),
            pltpu.VMEM((16, 16, LZ), F32),
            dma((3,)),
            dma((3,)),
            dma((8,)),
            dma((8,)),
            dma((8,)),
            dma((8,)),
            dma((8,)),
            dma((8,)),
            dma((3,)),
            dma((3,)),
        ],
        compiler_params=pltpu.CompilerParams(
            collective_id=0, has_side_effects=True, vmem_limit_bytes=48 << 20
        ),
        name="middle",
    )(main, tail, kernel_fine, kernel_coarse)
    bead, grid = pl.pallas_call(
        read_kernel,
        out_shape=(
            jax.ShapeDtypeStruct((1, slots), F32),
            jax.ShapeDtypeStruct((16, 16, LZ), F32),
        ),
        in_specs=[smem, vmem, vmem, vmem, vmem],
        out_specs=(vmem, vmem),
        scratch_shapes=[pltpu.VMEM((ROWS, 2 * LZ), BF16)],
        compiler_params=pltpu.CompilerParams(vmem_limit_bytes=40 << 20),
        name="read",
    )(bead_count, cells, weights, pmain, ptail)
    return (bead.reshape(1, 1, slots), grid)


def solution(mesh):
    sizes = (mesh.shape["gx"], mesh.shape["gy"])
    return jax.shard_map(
        functools.partial(on_device, sizes),
        mesh=mesh,
        in_specs=(
            P("gx", "gy", None),
            P("gx", "gy", None),
            P("gx", "gy"),
            P("gx", "gy", None, None),
            P(),
            P(),
        ),
        out_specs=(P("gx", "gy", None), P("gx", "gy", None)),
        check_vma=False,
    )
```

```python
import functools

import jax
import jax.numpy as jnp
from jax import lax
from jax.experimental import pallas as pl
from jax.experimental.pallas import tpu as pltpu
from jax.sharding import PartitionSpec as P

LX = 16
LY = 16
LZ = 128
SIDE = 17
BLOCK = 4096
ROWS = 384
STRIP = 1024
GROUP = 5
MESH = pl.DeviceIdType.MESH
F32 = jnp.float32
BF16 = jnp.bfloat16
LANES_BOTH = (((1,), (1,)), ((), ()))
ROWS_BOTH = (((0,), (0,)), ((), ()))
AROUND = [(a, b) for a in (-1, 0, 1) for b in (-1, 0, 1) if (a, b) != (0, 0)]


def iota(shape, dim):
    return lax.broadcasted_iota(jnp.int32, shape, dim)


def split(value):
    high = value.astype(BF16)
    low = (value - high.astype(F32)).astype(BF16)
    return high, low


def bead_tables(cells, weights):
    count = cells.shape[1]
    first = cells >> 11
    second = (cells >> 7) & 15
    third = cells & 127
    rows = iota((24, count), 0)
    away_first = rows - first
    away_second = rows - second
    rows_first = jnp.zeros((24, count), F32)
    rows_second = jnp.zeros((24, count), F32)
    for tap in range(4):
        rows_first = jnp.where(away_first == tap, weights[tap : tap + 1], rows_first)
        rows_second = jnp.where(away_second == tap, weights[4 + tap : 5 + tap], rows_second)
    depth = jnp.zeros((LZ, count), F32)
    away = (iota((LZ, count), 0) - third) & 127
    for tap in range(4):
        depth = jnp.where(away == tap, weights[8 + tap : 9 + tap], depth)
    return rows_first, rows_second, depth.astype(BF16)


def melt_kernel(
    sizes,
    count_ref,
    charge_hbm,
    cell_hbm,
    weight_hbm,
    fine_hbm,
    coarse_hbm,
    bead_ref,
    grid_ref,
    charge_ref,
    cell_ref,
    weight_ref,
    fine_ref,
    coarse_ref,
    load_sem,
    all_first,
    all_second,
    all_depth,
    spread_total,
    main,
    tail,
    side_first,
    side_second,
    side_both,
    charges,
    out_edge,
    out_corner,
    in_edge,
    in_corner,
    grid,
    operand,
    summed,
    lines,
    fine_strips,
    coarse_strips,
    out_coarse,
    in_coarse,
    wide_coarse,
    total,
    own_pot,
    out_pot,
    in_pot,
    wide_pot,
    rows_pot,
    send_tail,
    potential,
    upper_first,
    upper_second,
    upper_both,
    read_table,
    send_1,
    recv_1,
    send_2,
    recv_2,
    send_3,
    recv_3,
    send_4,
    recv_4,
    send_5,
    recv_5,
):
    here_first = lax.axis_index("gx")
    here_second = lax.axis_index("gy")
    live = count_ref[0, 0]

    def device(a, b):
        return (
            lax.rem(here_first + (a + sizes[0]), sizes[0]),
            lax.rem(here_second + (b + sizes[1]), sizes[1]),
        )

    def send(source, target, out_sem, in_sem, a, b):
        copy = pltpu.make_async_remote_copy(
            src_ref=source,
            dst_ref=target,
            send_sem=out_sem,
            recv_sem=in_sem,
            device_id=device(a, b),
            device_id_type=MESH,
        )
        copy.start()
        return copy

    loads = []
    for at, (source, target) in enumerate(
        [
            (cell_hbm, cell_ref),
            (weight_hbm, weight_ref),
            (charge_hbm, charge_ref),
            (fine_hbm, fine_ref),
            (coarse_hbm, coarse_ref),
        ]
    ):
        load = pltpu.make_async_copy(source, target, load_sem.at[at])
        load.start()
        loads.append(load)

    barrier = pltpu.get_barrier_semaphore()
    for a, b in AROUND:
        pl.semaphore_signal(barrier, inc=1, device_id=device(a, b), device_id_type=MESH)

    for load in loads:
        load.wait()

    spread_total[...] = jnp.zeros_like(spread_total)

    def add_block(step, carry):
        start = pl.multiple_of(step * BLOCK, BLOCK)
        here = pl.ds(start, BLOCK)
        slots = iota((1, BLOCK), 1) + start
        charge = jnp.where(slots < live, charge_ref[:, here], 0.0)
        weights = weight_ref[:, here].astype(F32)
        rows_first, rows_second, depth = bead_tables(cell_ref[:, here], weights)
        all_first[:, here] = rows_first
        all_second[:, here] = rows_second
        all_depth[:, here] = depth
        rows_first = rows_first * charge
        parts = [rows_first[x : x + 1] * rows_second[:16] for x in range(19)]
        parts += [rows_second[y : y + 1] * rows_first for y in range(16, 19)]
        parts += [jnp.zeros((8, BLOCK), F32)]
        high, low = split(jnp.concatenate(parts, axis=0))
        spread_total[...] += lax.dot_general(
            high, depth, LANES_BOTH, preferred_element_type=F32
        ) + lax.dot_general(low, depth, LANES_BOTH, preferred_element_type=F32)
        return carry

    lax.fori_loop(0, charge_ref.shape[1] // BLOCK, add_block, 0)
    main[...] = spread_total[0:304].reshape(19, 16, LZ)
    tail[...] = spread_total[304:376].reshape(3, 24, LZ)

    pl.semaphore_wait(barrier, 8)

    spills = [
        send(main.at[16:19], side_first, send_1.at[0], recv_1.at[0], 1, 0),
        send(tail.at[:, 16:24], side_both, send_1.at[2], recv_1.at[2], 1, 1),
        send(tail.at[:, 0:16], side_second, send_1.at[1], recv_1.at[1], 0, 1),
    ]

    lanes = iota((SIDE, LZ), 1)
    taps = iota((SIDE, LZ), 0)
    for at, source in enumerate((fine_ref, coarse_ref)):
        whole = [jnp.zeros((SIDE, LZ), F32)] * 2
        for chunk in range(5):
            placed = jnp.zeros((SIDE, LZ), F32)
            for j in range(4):
                dx = 4 * chunk + j
                if dx < SIDE:
                    place = (lanes == taps + 32 * j).astype(BF16)
                    placed = placed + lax.dot_general(
                        source[dx], place, ROWS_BOTH, preferred_element_type=F32
                    )
            whole.append(placed)
        whole = jnp.concatenate(whole + [jnp.zeros((SIDE, LZ), F32)], axis=1)
        for v in range(4):
            moved = whole if v == 0 else pltpu.roll(whole, STRIP - 32 * v, 1)
            for chunk in range(1, 7):
                lines[at, v, chunk, 0:SIDE] = moved[:, 128 * chunk : 128 * chunk + 128]

    for strips in (fine_strips, coarse_strips):
        strips[:, :, :, 0:128] = jnp.zeros((SIDE, 4, 16, 128), BF16)
        strips[:, :, :, 896:1024] = jnp.zeros((SIDE, 4, 16, 128), BF16)
        strips[:, 0, :, 128:256] = jnp.zeros((SIDE, 16, 128), BF16)
        strips[:, 1:4, :, 768:896] = jnp.zeros((SIDE, 3, 16, 128), BF16)

    def build(dz, carry):
        for at, strips in enumerate((fine_strips, coarse_strips)):
            for v in range(4):
                for chunk in range(2, 7) if v == 0 else range(1, 6):
                    span = slice(128 * chunk, 128 * chunk + 128)
                    line = lines[at, v, chunk, pl.ds(dz, 1)]
                    upper = pltpu.roll(
                        jnp.broadcast_to(line, (8, LZ)), 0, 1, stride=1, stride_axis=0
                    )
                    both = jnp.concatenate([upper, pltpu.roll(upper, 8, 1)], axis=0)
                    strips[dz, v, :, span] = both.astype(BF16)
        return carry

    lax.fori_loop(0, SIDE, build, 0)

    for copy in spills:
        copy.wait()
    charges[...] = main[0:16]
    charges[0:3] += side_first[...]
    for y in range(3):
        side_second[y, 0:8] += side_both[y]
        charges[:, y, :] += side_second[y]
    grid[8:24, 8:24] = charges[...].astype(BF16).astype(F32)

    out_edge[0] = grid[8:16, 8:24].astype(BF16)
    out_edge[1] = grid[16:24, 8:24].astype(BF16)
    out_edge[2] = grid[8:24, 8:16].reshape(8, 16, LZ).astype(BF16)
    out_edge[3] = grid[8:24, 16:24].reshape(8, 16, LZ).astype(BF16)
    for i in range(2):
        for j in range(2):
            quarter = grid[8 + 8 * i : 16 + 8 * i, 8 + 8 * j : 16 + 8 * j]
            out_corner[2 * i + j] = quarter.reshape(4, 16, LZ).astype(BF16)
    halos = []
    for at, (a, b) in enumerate([(-1, 0), (1, 0), (0, -1), (0, 1)]):
        halos.append(send(out_edge.at[at], in_edge.at[at], send_2.at[at], recv_2.at[at], a, b))
    for at, (a, b) in enumerate([(-1, -1), (-1, 1), (1, -1), (1, 1)]):
        halos.append(
            send(out_corner.at[at], in_corner.at[at], send_2.at[4 + at], recv_2.at[4 + at], a, b)
        )
    for copy in halos:
        copy.wait()
    grid[24:32, 8:24] = in_edge[0].astype(F32)
    grid[0:8, 8:24] = in_edge[1].astype(F32)
    grid[8:24, 24:32] = in_edge[2].astype(F32).reshape(16, 8, LZ)
    grid[8:24, 0:8] = in_edge[3].astype(F32).reshape(16, 8, LZ)
    for i in range(2):
        for j in range(2):
            quarter = in_corner[2 * i + j].astype(F32).reshape(8, 8, LZ)
            grid[24 - 24 * i : 32 - 24 * i, 24 - 24 * j : 32 - 24 * j] = quarter

    gap = (iota((LZ, LZ), 0) - 2 * (iota((LZ, LZ), 1) & 63) + 2) & 127
    spline = jnp.where(gap == 2, 0.75, 0.0)
    spline = jnp.where((gap == 1) | (gap == 3), 0.5, spline)
    spline = jnp.where((gap == 0) | (gap == 4), 0.125, spline).astype(BF16)
    coarse_lines = jnp.dot(
        grid[6:25].reshape(19 * 32, LZ).astype(BF16), spline, preferred_element_type=F32
    ).reshape(19, 32, LZ)
    for i in range(8):
        summed[i] = (
            0.125 * (coarse_lines[2 * i] + coarse_lines[2 * i + 4])
            + 0.5 * (coarse_lines[2 * i + 1] + coarse_lines[2 * i + 3])
            + 0.75 * coarse_lines[2 * i + 2]
        )
    lower = iota((8, LZ), 1) < 64
    wide_coarse[:, 24:32] = jnp.zeros((24, 8, LZ), F32)
    planes = []
    for i in range(8):
        parts = [summed[i, pl.ds(6 + t, 8, stride=2)] for t in range(5)]
        plane = 0.125 * (parts[0] + parts[4]) + 0.5 * (parts[1] + parts[3]) + 0.75 * parts[2]
        planes.append(plane.astype(BF16).astype(F32))
    pairs = [jnp.where(lower, planes[2 * j], planes[2 * j + 1]) for j in range(4)]
    for k in range(2):
        out_coarse[k] = jnp.concatenate(pairs[2 * k : 2 * k + 2], axis=0).astype(BF16)
    coarse_sends = []
    for at, (a, b) in enumerate(AROUND):
        coarse_sends.append(send(out_coarse, in_coarse.at[at], send_3.at[at], recv_3.at[at], a, b))
    for i in range(8):
        wide_coarse[8 + i, 8:16] = planes[i]

    def strip_rows(strips, dz):
        columns = []
        for q in range(3):
            blocks = []
            for x in range(8):
                a, v = divmod(8 - x + 8 * q, 4)
                blocks.append(strips[dz, v, :, 128 * a : 128 * a + 256])
            columns.append(jnp.concatenate(blocks, axis=0))
        return jnp.concatenate(columns, axis=1)

    operand[:, 0:LZ] = grid[0:24].reshape(768, LZ).astype(BF16)
    operand[:, LZ:] = grid[8:32].reshape(768, LZ).astype(BF16)
    total[...] = jnp.zeros_like(total)

    def products(strips, right, group):
        rows = jnp.concatenate([strip_rows(strips, dz) for dz in group], axis=0)
        result = jnp.dot(rows, right, preferred_element_type=F32)
        return [result[128 * at : 128 * at + 128] for at in range(len(group))]

    def turned(value, dz):
        return value if dz == 8 else pltpu.roll(value, (136 - dz) % 128, 1)

    def correlate_fine(first, last):
        for start in range(first, last, GROUP):
            group = range(start, min(start + GROUP, last))
            for dz, product in zip(group, products(fine_strips, operand[...], group)):
                total[0] += turned(product[:, :LZ], dz)
                total[1] += turned(product[:, LZ:], dz)

    correlate_fine(0, 9)

    for copy in coarse_sends:
        copy.wait()
    for at, (a, b) in enumerate(AROUND):
        for k in range(2):
            pair_rows = in_coarse[at, k].astype(F32)
            for j in range(2):
                pair = pair_rows[8 * j : 8 * j + 8]
                other = pltpu.roll(pair, 64, 1)
                x = 8 - 8 * a + 4 * k + 2 * j
                wide_coarse[x, 8 - 8 * b : 16 - 8 * b] = jnp.where(lower, pair, other)
                wide_coarse[x + 1, 8 - 8 * b : 16 - 8 * b] = jnp.where(lower, other, pair)
    coarse_operand = wide_coarse[...].reshape(768, LZ).astype(BF16)
    own_pot[...] = jnp.zeros_like(own_pot)

    for start in range(0, SIDE, GROUP):
        group = range(start, min(start + GROUP, SIDE))
        for dz, product in zip(group, products(coarse_strips, coarse_operand, group)):
            near = product.reshape(8, 16, LZ)[:, 0:8].reshape(64, LZ)
            own_pot[...] += turned(near, dz).reshape(8, 8, LZ)

    out_pot[0] = own_pot[:, 0, :]
    out_pot[1] = own_pot[:, 7, :]
    pot_sends = []
    for at, (a, b) in enumerate(AROUND):
        if a == 0:
            source = out_pot.at[0 if b < 0 else 1]
        else:
            source = own_pot.at[0 if a < 0 else 7]
        pot_sends.append(send(source, in_pot.at[at], send_4.at[at], recv_4.at[at], a, b))

    correlate_fine(9, SIDE)

    for copy in pot_sends:
        copy.wait()
    wide_pot[1:9, 8:16] = own_pot[...]
    for at, (a, b) in enumerate(AROUND):
        if a == 0:
            wide_pot[1:9, 16 if b < 0 else 7, :] = in_pot[at]
        else:
            wide_pot[9 if a < 0 else 0, 8 - 8 * b : 16 - 8 * b] = in_pot[at]
    for i in range(8):
        rows_pot[2 * i] = (wide_pot[i] + 6.0 * wide_pot[i + 1] + wide_pot[i + 2]) * 0.125
        rows_pot[2 * i + 1] = (wide_pot[i + 1] + wide_pot[i + 2]) * 0.5
    below = rows_pot[:, 7:15]
    middle = rows_pot[:, 8:16]
    above = rows_pot[:, 9:17]
    even_rows = (below + 6.0 * middle + above) * 0.125
    odd_rows = (middle + above) * 0.5
    for i in range(16):
        potential[i, pl.ds(0, 8, stride=2)] = even_rows[i]
        potential[i, pl.ds(1, 8, stride=2)] = odd_rows[i]
    source = iota((LZ, LZ), 0)
    offset = (iota((LZ, LZ), 1) - 2 * source + 2) & 127
    refine = jnp.where(offset == 2, 0.75, 0.0)
    refine = jnp.where((offset == 1) | (offset == 3), 0.5, refine)
    refine = jnp.where((offset == 0) | (offset == 4), 0.125, refine)
    refine = jnp.where(source < 64, refine, 0.0).astype(BF16)
    high, low = split(potential[...].reshape(256, LZ))
    smooth = jnp.dot(
        jnp.concatenate([high, low], axis=1),
        jnp.concatenate([refine, refine], axis=0),
        preferred_element_type=F32,
    )
    potential[...] = (total[...].reshape(256, LZ) + smooth).reshape(16, 16, LZ)

    for y in range(3):
        send_tail[y] = potential[:, y, :]
    upper = [
        send(potential.at[0:3], upper_first, send_5.at[0], recv_5.at[0], -1, 0),
        send(send_tail.at[:, 0:8], upper_both, send_5.at[2], recv_5.at[2], -1, -1),
        send(send_tail, upper_second, send_5.at[1], recv_5.at[1], 0, -1),
    ]
    grid_ref[...] = potential[...]

    def put_table(start, rows):
        high, low = split(rows)
        read_table[start : start + rows.shape[0], 0:LZ] = high
        read_table[start : start + rows.shape[0], LZ:] = low

    put_table(0, potential[...].reshape(256, LZ))
    for copy in upper:
        copy.wait()
    put_table(256, upper_first[...].reshape(48, LZ))
    ends = []
    for y in range(3):
        ends += [upper_second[y], upper_both[y]]
    ends += [jnp.zeros((8, LZ), F32)]
    put_table(304, jnp.concatenate(ends, axis=0))

    def read_block(step, carry):
        start = pl.multiple_of(step * BLOCK, BLOCK)
        here = pl.ds(start, BLOCK)
        rows_first = all_first[:, here]
        rows_second = all_second[:, here]
        depth = all_depth[:, here]
        along = jnp.dot(
            read_table[...], jnp.concatenate([depth, depth], axis=0), preferred_element_type=F32
        )
        near = jnp.zeros((16, BLOCK), F32)
        for x in range(19):
            near = near + rows_first[x : x + 1] * along[16 * x : 16 * x + 16]
        far = jnp.zeros((24, BLOCK), F32)
        for y in range(3):
            far = far + rows_second[16 + y : 17 + y] * along[304 + 24 * y : 328 + 24 * y]
        near = near * rows_second[:16]
        far = far * rows_first
        both = near[:8] + near[8:] + far[:8] + far[8:16] + far[16:]
        slots = iota((1, BLOCK), 1) + start
        value = jnp.sum(both, axis=0, keepdims=True)
        bead_ref[:, here] = jnp.where(slots < live, value, 0.0)
        return carry

    lax.fori_loop(0, cell_ref.shape[1] // BLOCK, read_block, 0)


def on_device(sizes, bead_charge, bead_cell, bead_count, interp_weights, kernel_fine, kernel_coarse):
    slots = bead_charge.shape[-1]
    charge = bead_charge.reshape(1, slots)
    cells = bead_cell.reshape(1, slots)
    weights = interp_weights.reshape(12, slots)
    vmem = pl.BlockSpec(memory_space=pltpu.VMEM)
    smem = pl.BlockSpec(memory_space=pltpu.SMEM)
    anywhere = pl.BlockSpec(memory_space=pl.ANY)
    dma = pltpu.SemaphoreType.DMA
    scratch = [
        pltpu.VMEM((1, slots), F32),
        pltpu.VMEM((1, slots), jnp.int32),
        pltpu.VMEM((12, slots), BF16),
        pltpu.VMEM((SIDE, SIDE, SIDE), BF16),
        pltpu.VMEM((SIDE, SIDE, SIDE), BF16),
        dma((5,)),
        pltpu.VMEM((24, slots), F32),
        pltpu.VMEM((24, slots), F32),
        pltpu.VMEM((LZ, slots), BF16),
        pltpu.VMEM((ROWS, LZ), F32),
        pltpu.VMEM((19, 16, LZ), F32),
        pltpu.VMEM((3, 24, LZ), F32),
        pltpu.VMEM((3, 16, LZ), F32),
        pltpu.VMEM((3, 16, LZ), F32),
        pltpu.VMEM((3, 8, LZ), F32),
        pltpu.VMEM((16, 16, LZ), F32),
        pltpu.VMEM((4, 8, 16, LZ), BF16),
        pltpu.VMEM((4, 4, 16, LZ), BF16),
        pltpu.VMEM((4, 8, 16, LZ), BF16),
        pltpu.VMEM((4, 4, 16, LZ), BF16),
        pltpu.VMEM((32, 32, LZ), F32),
        pltpu.VMEM((768, 2 * LZ), BF16),
        pltpu.VMEM((8, 32, LZ), F32),
        pltpu.VMEM((2, 4, 8, 24, LZ), F32),
        pltpu.VMEM((SIDE, 4, 16, STRIP), BF16),
        pltpu.VMEM((SIDE, 4, 16, STRIP), BF16),
        pltpu.VMEM((2, 16, LZ), BF16),
        pltpu.VMEM((8, 2, 16, LZ), BF16),
        pltpu.VMEM((24, 32, LZ), F32),
        pltpu.VMEM((2, LZ, LZ), F32),
        pltpu.VMEM((8, 8, LZ), F32),
        pltpu.VMEM((2, 8, LZ), F32),
        pltpu.VMEM((8, 8, LZ), F32),
        pltpu.VMEM((10, 24, LZ), F32),
        pltpu.VMEM((16, 24, LZ), F32),
        pltpu.VMEM((3, 16, LZ), F32),
        pltpu.VMEM((16, 16, LZ), F32),
        pltpu.VMEM((3, 16, LZ), F32),
        pltpu.VMEM((3, 16, LZ), F32),
        pltpu.VMEM((3, 8, LZ), F32),
        pltpu.VMEM((ROWS, 2 * LZ), BF16),
    ]
    for count in (3, 8, 8, 8, 3):
        scratch += [dma((count,)), dma((count,))]
    bead, grid = pl.pallas_call(
        functools.partial(melt_kernel, sizes),
        out_shape=(
            jax.ShapeDtypeStruct((1, slots), F32),
            jax.ShapeDtypeStruct((16, 16, LZ), F32),
        ),
        in_specs=[smem] + [anywhere] * 5,
        out_specs=(vmem, vmem),
        scratch_shapes=scratch,
        compiler_params=pltpu.CompilerParams(
            collective_id=0, has_side_effects=True, vmem_limit_bytes=60 << 20
        ),
        name="melt",
    )(bead_count, charge, cells, weights, kernel_fine, kernel_coarse)
    return (bead.reshape(1, 1, slots), grid)


def solution(mesh):
    sizes = (mesh.shape["gx"], mesh.shape["gy"])
    return jax.shard_map(
        functools.partial(on_device, sizes),
        mesh=mesh,
        in_specs=(
            P("gx", "gy", None),
            P("gx", "gy", None),
            P("gx", "gy"),
            P("gx", "gy", None, None),
            P(),
            P(),
        ),
        out_specs=(P("gx", "gy", None), P("gx", "gy", None)),
        check_vma=False,
    )
```

```python
import functools

import jax
import jax.numpy as jnp
from jax import lax
from jax.experimental import pallas as pl
from jax.experimental.pallas import tpu as pltpu
from jax.sharding import PartitionSpec as P

LX = 16
LY = 16
LZ = 128
SIDE = 17
BLOCK = 8192
ROWS = 384
STRIP = 1024
GROUP = 5
MESH = pl.DeviceIdType.MESH
F32 = jnp.float32
BF16 = jnp.bfloat16
LANES_BOTH = (((1,), (1,)), ((), ()))
ROWS_BOTH = (((0,), (0,)), ((), ()))
AROUND = [(a, b) for a in (-1, 0, 1) for b in (-1, 0, 1) if (a, b) != (0, 0)]


def iota(shape, dim):
    return lax.broadcasted_iota(jnp.int32, shape, dim)


def split(value):
    high = value.astype(BF16)
    low = (value - high.astype(F32)).astype(BF16)
    return high, low


def bead_tables(cells, weights):
    count = cells.shape[1]
    first = cells >> 11
    second = (cells >> 7) & 15
    third = cells & 127
    rows = iota((24, count), 0)
    away_first = rows - first
    away_second = rows - second
    rows_first = jnp.zeros((24, count), F32)
    rows_second = jnp.zeros((24, count), F32)
    for tap in range(4):
        rows_first = jnp.where(away_first == tap, weights[tap : tap + 1], rows_first)
        rows_second = jnp.where(away_second == tap, weights[4 + tap : 5 + tap], rows_second)
    depth = jnp.zeros((LZ, count), BF16)
    places = iota((LZ, count), 0).astype(F32).astype(BF16)
    for tap in range(4):
        target = ((third + tap) & 127).astype(F32).astype(BF16)
        depth = jnp.where(places == target, weights[8 + tap : 9 + tap].astype(BF16), depth)
    return rows_first, rows_second, depth


def melt_kernel(
    sizes,
    count_ref,
    charge_hbm,
    cell_hbm,
    weight_hbm,
    fine_hbm,
    coarse_hbm,
    bead_ref,
    grid_ref,
    charge_ref,
    cell_ref,
    weight_ref,
    fine_ref,
    coarse_ref,
    load_sem,
    all_first,
    all_second,
    all_depth,
    far_total,
    near_total,
    main_far,
    tail,
    side_first,
    side_second,
    side_both,
    charges,
    out_edge,
    out_corner,
    in_edge,
    in_corner,
    grid,
    operand,
    summed,
    lines,
    fine_strips,
    coarse_strips,
    out_coarse,
    in_coarse,
    wide_coarse,
    total,
    own_pot,
    out_pot,
    in_pot,
    wide_pot,
    rows_pot,
    send_tail,
    potential,
    upper_first,
    upper_second,
    upper_both,
    read_table,
    send_1,
    recv_1,
    send_2,
    recv_2,
    send_3,
    recv_3,
    send_4,
    recv_4,
    send_5,
    recv_5,
):
    here_first = lax.axis_index("gx")
    here_second = lax.axis_index("gy")
    live = count_ref[0, 0]

    def device(a, b):
        return (
            lax.rem(here_first + (a + sizes[0]), sizes[0]),
            lax.rem(here_second + (b + sizes[1]), sizes[1]),
        )

    def send(source, target, out_sem, in_sem, a, b):
        copy = pltpu.make_async_remote_copy(
            src_ref=source,
            dst_ref=target,
            send_sem=out_sem,
            recv_sem=in_sem,
            device_id=device(a, b),
            device_id_type=MESH,
        )
        copy.start()
        return copy

    loads = []
    for at, (source, target) in enumerate(
        [
            (cell_hbm, cell_ref),
            (weight_hbm, weight_ref),
            (charge_hbm, charge_ref),
            (fine_hbm, fine_ref),
            (coarse_hbm, coarse_ref),
        ]
    ):
        load = pltpu.make_async_copy(source, target, load_sem.at[at])
        load.start()
        loads.append(load)

    barrier = pltpu.get_barrier_semaphore()
    for a, b in AROUND:
        pl.semaphore_signal(barrier, inc=1, device_id=device(a, b), device_id_type=MESH)

    for load in loads:
        load.wait()

    far_total[...] = jnp.zeros_like(far_total)
    near_total[...] = jnp.zeros_like(near_total)

    def block_at(step):
        start = pl.multiple_of(step * BLOCK, BLOCK)
        return pl.ds(start, BLOCK), iota((1, BLOCK), 1) + start < live

    def add_rows(sums, parts, depth):
        high, low = split(jnp.concatenate(parts, axis=0))
        both = lax.dot_general(
            jnp.concatenate([high, low], axis=0), depth, LANES_BOTH, preferred_element_type=F32
        )
        sums[...] += both[: high.shape[0]] + both[high.shape[0] :]

    def spread_far(step, carry):
        here, alive = block_at(step)
        weights = weight_ref[:, here].astype(F32)
        rows_first, rows_second, depth = bead_tables(cell_ref[:, here], weights)
        all_first[:, here] = rows_first
        all_second[:, here] = rows_second
        all_depth[:, here] = depth
        rows_first = rows_first * jnp.where(alive, charge_ref[:, here], 0.0)
        parts = [rows_first[x : x + 1] * rows_second[:16] for x in range(16, 19)]
        parts += [rows_second[y : y + 1] * rows_first for y in range(16, 19)]
        parts += [jnp.zeros((8, BLOCK), F32)]
        add_rows(far_total, parts, depth)
        return carry

    def spread_near(step, carry):
        here, alive = block_at(step)
        rows_first = all_first[0:16, here] * jnp.where(alive, charge_ref[:, here], 0.0)
        rows_second = all_second[0:16, here]
        parts = [rows_first[x : x + 1] * rows_second for x in range(16)]
        add_rows(near_total, parts, all_depth[:, here])
        return carry

    steps = charge_ref.shape[1] // BLOCK
    lax.fori_loop(0, steps, spread_far, 0)
    main_far[...] = far_total[0:48].reshape(3, 16, LZ)
    tail[...] = far_total[48:120].reshape(3, 24, LZ)

    pl.semaphore_wait(barrier, 8)

    spills = [
        send(main_far, side_first, send_1.at[0], recv_1.at[0], 1, 0),
        send(tail.at[:, 16:24], side_both, send_1.at[2], recv_1.at[2], 1, 1),
        send(tail.at[:, 0:16], side_second, send_1.at[1], recv_1.at[1], 0, 1),
    ]

    lax.fori_loop(0, steps, spread_near, 0)

    for copy in spills:
        copy.wait()
    charges[...] = near_total[...].reshape(16, 16, LZ)
    charges[0:3] += side_first[...]
    for y in range(3):
        side_second[y, 0:8] += side_both[y]
        charges[:, y, :] += side_second[y]
    grid[8:24, 8:24] = charges[...].astype(BF16).astype(F32)

    out_edge[0] = grid[8:16, 8:24].astype(BF16)
    out_edge[1] = grid[16:24, 8:24].astype(BF16)
    out_edge[2] = grid[8:24, 8:16].reshape(8, 16, LZ).astype(BF16)
    out_edge[3] = grid[8:24, 16:24].reshape(8, 16, LZ).astype(BF16)
    for i in range(2):
        for j in range(2):
            quarter = grid[8 + 8 * i : 16 + 8 * i, 8 + 8 * j : 16 + 8 * j]
            out_corner[2 * i + j] = quarter.reshape(4, 16, LZ).astype(BF16)
    halos = []
    for at, (a, b) in enumerate([(-1, 0), (1, 0), (0, -1), (0, 1)]):
        halos.append(send(out_edge.at[at], in_edge.at[at], send_2.at[at], recv_2.at[at], a, b))
    for at, (a, b) in enumerate([(-1, -1), (-1, 1), (1, -1), (1, 1)]):
        halos.append(
            send(out_corner.at[at], in_corner.at[at], send_2.at[4 + at], recv_2.at[4 + at], a, b)
        )
    lanes = iota((SIDE, LZ), 1)
    taps = iota((SIDE, LZ), 0)
    for at, source in enumerate((fine_ref, coarse_ref)):
        whole = [jnp.zeros((SIDE, LZ), F32)] * 2
        for chunk in range(5):
            placed = jnp.zeros((SIDE, LZ), F32)
            for j in range(4):
                dx = 4 * chunk + j
                if dx < SIDE:
                    place = (lanes == taps + 32 * j).astype(BF16)
                    placed = placed + lax.dot_general(
                        source[dx], place, ROWS_BOTH, preferred_element_type=F32
                    )
            whole.append(placed)
        whole = jnp.concatenate(whole + [jnp.zeros((SIDE, LZ), F32)], axis=1)
        for v in range(4):
            moved = whole if v == 0 else pltpu.roll(whole, STRIP - 32 * v, 1)
            for chunk in range(1, 7):
                lines[at, v, chunk, 0:SIDE] = moved[:, 128 * chunk : 128 * chunk + 128]

    for strips in (fine_strips, coarse_strips):
        strips[:, :, :, 0:128] = jnp.zeros((SIDE, 4, 16, 128), BF16)
        strips[:, :, :, 896:1024] = jnp.zeros((SIDE, 4, 16, 128), BF16)
        strips[:, 0, :, 128:256] = jnp.zeros((SIDE, 16, 128), BF16)
        strips[:, 1:4, :, 768:896] = jnp.zeros((SIDE, 3, 16, 128), BF16)

    def build(dz, carry):
        for at, strips in enumerate((fine_strips, coarse_strips)):
            for v in range(4):
                for chunk in range(2, 7) if v == 0 else range(1, 6):
                    span = slice(128 * chunk, 128 * chunk + 128)
                    line = lines[at, v, chunk, pl.ds(dz, 1)]
                    upper = pltpu.roll(
                        jnp.broadcast_to(line, (8, LZ)), 0, 1, stride=1, stride_axis=0
                    )
                    both = jnp.concatenate([upper, pltpu.roll(upper, 8, 1)], axis=0)
                    strips[dz, v, :, span] = both.astype(BF16)
        return carry

    lax.fori_loop(0, SIDE, build, 0)

    for copy in halos:
        copy.wait()
    grid[24:32, 8:24] = in_edge[0].astype(F32)
    grid[0:8, 8:24] = in_edge[1].astype(F32)
    grid[8:24, 24:32] = in_edge[2].astype(F32).reshape(16, 8, LZ)
    grid[8:24, 0:8] = in_edge[3].astype(F32).reshape(16, 8, LZ)
    for i in range(2):
        for j in range(2):
            quarter = in_corner[2 * i + j].astype(F32).reshape(8, 8, LZ)
            grid[24 - 24 * i : 32 - 24 * i, 24 - 24 * j : 32 - 24 * j] = quarter

    gap = (iota((LZ, LZ), 0) - 2 * (iota((LZ, LZ), 1) & 63) + 2) & 127
    spline = jnp.where(gap == 2, 0.75, 0.0)
    spline = jnp.where((gap == 1) | (gap == 3), 0.5, spline)
    spline = jnp.where((gap == 0) | (gap == 4), 0.125, spline).astype(BF16)
    coarse_lines = jnp.dot(
        grid[6:25].reshape(19 * 32, LZ).astype(BF16), spline, preferred_element_type=F32
    ).reshape(19, 32, LZ)
    for i in range(8):
        summed[i] = (
            0.125 * (coarse_lines[2 * i] + coarse_lines[2 * i + 4])
            + 0.5 * (coarse_lines[2 * i + 1] + coarse_lines[2 * i + 3])
            + 0.75 * coarse_lines[2 * i + 2]
        )
    lower = iota((8, LZ), 1) < 64
    wide_coarse[:, 24:32] = jnp.zeros((24, 8, LZ), F32)
    planes = []
    for i in range(8):
        parts = [summed[i, pl.ds(6 + t, 8, stride=2)] for t in range(5)]
        plane = 0.125 * (parts[0] + parts[4]) + 0.5 * (parts[1] + parts[3]) + 0.75 * parts[2]
        planes.append(plane.astype(BF16).astype(F32))
    pairs = [jnp.where(lower, planes[2 * j], planes[2 * j + 1]) for j in range(4)]
    for k in range(2):
        out_coarse[k] = jnp.concatenate(pairs[2 * k : 2 * k + 2], axis=0).astype(BF16)
    coarse_sends = []
    for at, (a, b) in enumerate(AROUND):
        coarse_sends.append(send(out_coarse, in_coarse.at[at], send_3.at[at], recv_3.at[at], a, b))
    for i in range(8):
        wide_coarse[8 + i, 8:16] = planes[i]

    def strip_rows(strips, dz):
        columns = []
        for q in range(3):
            blocks = []
            for x in range(8):
                a, v = divmod(8 - x + 8 * q, 4)
                blocks.append(strips[dz, v, :, 128 * a : 128 * a + 256])
            columns.append(jnp.concatenate(blocks, axis=0))
        return jnp.concatenate(columns, axis=1)

    operand[:, 0:LZ] = grid[0:24].reshape(768, LZ).astype(BF16)
    operand[:, LZ:] = grid[8:32].reshape(768, LZ).astype(BF16)
    total[...] = jnp.zeros_like(total)

    def products(strips, right, group):
        rows = jnp.concatenate([strip_rows(strips, dz) for dz in group], axis=0)
        result = jnp.dot(rows, right, preferred_element_type=F32)
        return [result[128 * at : 128 * at + 128] for at in range(len(group))]

    def turned(value, dz):
        return value if dz == 8 else pltpu.roll(value, (136 - dz) % 128, 1)

    def correlate_fine(first, last):
        for start in range(first, last, GROUP):
            group = range(start, min(start + GROUP, last))
            for dz, product in zip(group, products(fine_strips, operand[...], group)):
                total[0] += turned(product[:, :LZ], dz)
                total[1] += turned(product[:, LZ:], dz)

    correlate_fine(0, 9)

    for copy in coarse_sends:
        copy.wait()
    for at, (a, b) in enumerate(AROUND):
        for k in range(2):
            pair_rows = in_coarse[at, k].astype(F32)
            for j in range(2):
                pair = pair_rows[8 * j : 8 * j + 8]
                other = pltpu.roll(pair, 64, 1)
                x = 8 - 8 * a + 4 * k + 2 * j
                wide_coarse[x, 8 - 8 * b : 16 - 8 * b] = jnp.where(lower, pair, other)
                wide_coarse[x + 1, 8 - 8 * b : 16 - 8 * b] = jnp.where(lower, other, pair)
    coarse_operand = wide_coarse[...].reshape(768, LZ).astype(BF16)
    own_pot[...] = jnp.zeros_like(own_pot)

    for start in range(0, SIDE, GROUP):
        group = range(start, min(start + GROUP, SIDE))
        for dz, product in zip(group, products(coarse_strips, coarse_operand, group)):
            near = product.reshape(8, 16, LZ)[:, 0:8].reshape(64, LZ)
            own_pot[...] += turned(near, dz).reshape(8, 8, LZ)

    out_pot[0] = own_pot[:, 0, :]
    out_pot[1] = own_pot[:, 7, :]
    pot_sends = []
    for at, (a, b) in enumerate(AROUND):
        if a == 0:
            source = out_pot.at[0 if b < 0 else 1]
        else:
            source = own_pot.at[0 if a < 0 else 7]
        pot_sends.append(send(source, in_pot.at[at], send_4.at[at], recv_4.at[at], a, b))

    correlate_fine(9, SIDE)

    for copy in pot_sends:
        copy.wait()
    wide_pot[1:9, 8:16] = own_pot[...]
    for at, (a, b) in enumerate(AROUND):
        if a == 0:
            wide_pot[1:9, 16 if b < 0 else 7, :] = in_pot[at]
        else:
            wide_pot[9 if a < 0 else 0, 8 - 8 * b : 16 - 8 * b] = in_pot[at]
    for i in range(8):
        rows_pot[2 * i] = (wide_pot[i] + 6.0 * wide_pot[i + 1] + wide_pot[i + 2]) * 0.125
        rows_pot[2 * i + 1] = (wide_pot[i + 1] + wide_pot[i + 2]) * 0.5
    below = rows_pot[:, 7:15]
    middle = rows_pot[:, 8:16]
    above = rows_pot[:, 9:17]
    even_rows = (below + 6.0 * middle + above) * 0.125
    odd_rows = (middle + above) * 0.5
    for i in range(16):
        potential[i, pl.ds(0, 8, stride=2)] = even_rows[i]
        potential[i, pl.ds(1, 8, stride=2)] = odd_rows[i]
    source = iota((LZ, LZ), 0)
    offset = (iota((LZ, LZ), 1) - 2 * source + 2) & 127
    refine = jnp.where(offset == 2, 0.75, 0.0)
    refine = jnp.where((offset == 1) | (offset == 3), 0.5, refine)
    refine = jnp.where((offset == 0) | (offset == 4), 0.125, refine)
    refine = jnp.where(source < 64, refine, 0.0).astype(BF16)
    high, low = split(potential[...].reshape(256, LZ))
    smooth = jnp.dot(
        jnp.concatenate([high, low], axis=1),
        jnp.concatenate([refine, refine], axis=0),
        preferred_element_type=F32,
    )
    potential[...] = (total[...].reshape(256, LZ) + smooth).reshape(16, 16, LZ)

    for y in range(3):
        send_tail[y] = potential[:, y, :]
    upper = [
        send(potential.at[0:3], upper_first, send_5.at[0], recv_5.at[0], -1, 0),
        send(send_tail.at[:, 0:8], upper_both, send_5.at[2], recv_5.at[2], -1, -1),
        send(send_tail, upper_second, send_5.at[1], recv_5.at[1], 0, -1),
    ]
    grid_ref[...] = potential[...]

    def put_table(start, rows):
        high, low = split(rows)
        read_table[start : start + rows.shape[0], 0:LZ] = high
        read_table[start : start + rows.shape[0], LZ:] = low

    put_table(0, potential[...].reshape(256, LZ))

    def read_near(step, carry):
        here, _ = block_at(step)
        depth = all_depth[:, here]
        along = jnp.dot(
            read_table[0:256], jnp.concatenate([depth, depth], axis=0), preferred_element_type=F32
        )
        rows_first = all_first[:, here]
        near = jnp.zeros((16, BLOCK), F32)
        for x in range(16):
            near = near + rows_first[x : x + 1] * along[16 * x : 16 * x + 16]
        near = near * all_second[0:16, here]
        bead_ref[:, here] = jnp.sum(near[:8] + near[8:], axis=0, keepdims=True)
        return carry

    lax.fori_loop(0, steps, read_near, 0)

    for copy in upper:
        copy.wait()
    put_table(256, upper_first[...].reshape(48, LZ))
    ends = []
    for y in range(3):
        ends += [upper_second[y], upper_both[y]]
    ends += [jnp.zeros((8, LZ), F32)]
    put_table(304, jnp.concatenate(ends, axis=0))

    def read_far(step, carry):
        here, alive = block_at(step)
        depth = all_depth[:, here]
        along = jnp.dot(
            read_table[256:384],
            jnp.concatenate([depth, depth], axis=0),
            preferred_element_type=F32,
        )
        rows_first = all_first[:, here]
        rows_second = all_second[:, here]
        near = jnp.zeros((16, BLOCK), F32)
        for x in range(3):
            near = near + rows_first[16 + x : 17 + x] * along[16 * x : 16 * x + 16]
        far = jnp.zeros((24, BLOCK), F32)
        for y in range(3):
            far = far + rows_second[16 + y : 17 + y] * along[48 + 24 * y : 72 + 24 * y]
        near = near * rows_second[:16]
        far = far * rows_first
        both = near[:8] + near[8:] + far[:8] + far[8:16] + far[16:]
        value = bead_ref[:, here] + jnp.sum(both, axis=0, keepdims=True)
        bead_ref[:, here] = jnp.where(alive, value, 0.0)
        return carry

    lax.fori_loop(0, steps, read_far, 0)


def hand_over(bead_from, grid_from, bead_to, grid_to):
    bead_to[...] = bead_from[...]
    grid_to[...] = grid_from[...]


def on_device(sizes, bead_charge, bead_cell, bead_count, interp_weights, kernel_fine, kernel_coarse):
    slots = bead_charge.shape[-1]
    charge = bead_charge.reshape(1, slots)
    cells = bead_cell.reshape(1, slots)
    weights = interp_weights.reshape(12, slots)
    vmem = pl.BlockSpec(memory_space=pltpu.VMEM)
    smem = pl.BlockSpec(memory_space=pltpu.SMEM)
    anywhere = pl.BlockSpec(memory_space=pl.ANY)
    dma = pltpu.SemaphoreType.DMA
    scratch = [
        pltpu.VMEM((1, slots), F32),
        pltpu.VMEM((1, slots), jnp.int32),
        pltpu.VMEM((12, slots), BF16),
        pltpu.VMEM((SIDE, SIDE, SIDE), BF16),
        pltpu.VMEM((SIDE, SIDE, SIDE), BF16),
        dma((5,)),
        pltpu.VMEM((24, slots), F32),
        pltpu.VMEM((24, slots), F32),
        pltpu.VMEM((LZ, slots), BF16),
        pltpu.VMEM((128, LZ), F32),
        pltpu.VMEM((256, LZ), F32),
        pltpu.VMEM((3, 16, LZ), F32),
        pltpu.VMEM((3, 24, LZ), F32),
        pltpu.VMEM((3, 16, LZ), F32),
        pltpu.VMEM((3, 16, LZ), F32),
        pltpu.VMEM((3, 8, LZ), F32),
        pltpu.VMEM((16, 16, LZ), F32),
        pltpu.VMEM((4, 8, 16, LZ), BF16),
        pltpu.VMEM((4, 4, 16, LZ), BF16),
        pltpu.VMEM((4, 8, 16, LZ), BF16),
        pltpu.VMEM((4, 4, 16, LZ), BF16),
        pltpu.VMEM((32, 32, LZ), F32),
        pltpu.VMEM((768, 2 * LZ), BF16),
        pltpu.VMEM((8, 32, LZ), F32),
        pltpu.VMEM((2, 4, 8, 24, LZ), F32),
        pltpu.VMEM((SIDE, 4, 16, STRIP), BF16),
        pltpu.VMEM((SIDE, 4, 16, STRIP), BF16),
        pltpu.VMEM((2, 16, LZ), BF16),
        pltpu.VMEM((8, 2, 16, LZ), BF16),
        pltpu.VMEM((24, 32, LZ), F32),
        pltpu.VMEM((2, LZ, LZ), F32),
        pltpu.VMEM((8, 8, LZ), F32),
        pltpu.VMEM((2, 8, LZ), F32),
        pltpu.VMEM((8, 8, LZ), F32),
        pltpu.VMEM((10, 24, LZ), F32),
        pltpu.VMEM((16, 24, LZ), F32),
        pltpu.VMEM((3, 16, LZ), F32),
        pltpu.VMEM((16, 16, LZ), F32),
        pltpu.VMEM((3, 16, LZ), F32),
        pltpu.VMEM((3, 16, LZ), F32),
        pltpu.VMEM((3, 8, LZ), F32),
        pltpu.VMEM((ROWS, 2 * LZ), BF16),
    ]
    for count in (3, 8, 8, 8, 3):
        scratch += [dma((count,)), dma((count,))]
    bead, grid = pl.pallas_call(
        functools.partial(melt_kernel, sizes),
        out_shape=(
            jax.ShapeDtypeStruct((1, slots), F32),
            jax.ShapeDtypeStruct((16, 16, LZ), F32),
        ),
        in_specs=[smem] + [anywhere] * 5,
        out_specs=(vmem, vmem),
        scratch_shapes=scratch,
        compiler_params=pltpu.CompilerParams(
            collective_id=0, has_side_effects=True, vmem_limit_bytes=60 << 20
        ),
        name="melt",
    )(bead_count, charge, cells, weights, kernel_fine, kernel_coarse)
    bead, grid = pl.pallas_call(
        hand_over,
        out_shape=(
            jax.ShapeDtypeStruct((1, slots), F32),
            jax.ShapeDtypeStruct((16, 16, LZ), F32),
        ),
        in_specs=[vmem, vmem],
        out_specs=(vmem, vmem),
        name="hand_over",
    )(bead, grid)
    return (bead.reshape(1, 1, slots), grid)


def solution(mesh):
    sizes = (mesh.shape["gx"], mesh.shape["gy"])
    return jax.shard_map(
        functools.partial(on_device, sizes),
        mesh=mesh,
        in_specs=(
            P("gx", "gy", None),
            P("gx", "gy", None),
            P("gx", "gy"),
            P("gx", "gy", None, None),
            P(),
            P(),
        ),
        out_specs=(P("gx", "gy", None), P("gx", "gy", None)),
        check_vma=False,
    )
```

```python
import functools

import jax
import jax.numpy as jnp
from jax import lax
from jax.experimental import pallas as pl
from jax.experimental.pallas import tpu as pltpu
from jax.sharding import PartitionSpec as P

LX = 16
LY = 16
LZ = 128
SIDE = 17
BLOCK = 8192
ROWS = 384
STRIP = 1024
GROUP = 5
MESH = pl.DeviceIdType.MESH
F32 = jnp.float32
BF16 = jnp.bfloat16
LANES_BOTH = (((1,), (1,)), ((), ()))
ROWS_BOTH = (((0,), (0,)), ((), ()))
AROUND = [(a, b) for a in (-1, 0, 1) for b in (-1, 0, 1) if (a, b) != (0, 0)]


def iota(shape, dim):
    return lax.broadcasted_iota(jnp.int32, shape, dim)


def split(value):
    high = value.astype(BF16)
    low = (value - high.astype(F32)).astype(BF16)
    return high, low


def bead_tables(cells, weights):
    count = cells.shape[1]
    first = cells >> 11
    second = (cells >> 7) & 15
    third = cells & 127
    rows = iota((24, count), 0)
    away_first = rows - first
    away_second = rows - second
    rows_first = jnp.zeros((24, count), F32)
    rows_second = jnp.zeros((24, count), F32)
    for tap in range(4):
        rows_first = jnp.where(away_first == tap, weights[tap : tap + 1], rows_first)
        rows_second = jnp.where(away_second == tap, weights[4 + tap : 5 + tap], rows_second)
    depth = jnp.zeros((LZ, count), BF16)
    places = iota((LZ, count), 0).astype(F32).astype(BF16)
    for tap in range(4):
        target = ((third + tap) & 127).astype(F32).astype(BF16)
        depth = jnp.where(places == target, weights[8 + tap : 9 + tap].astype(BF16), depth)
    return rows_first, rows_second, depth


def melt_kernel(
    sizes,
    count_ref,
    charge_hbm,
    cell_hbm,
    weight_hbm,
    fine_hbm,
    coarse_hbm,
    bead_ref,
    grid_ref,
    charge_ref,
    cell_ref,
    weight_ref,
    fine_ref,
    coarse_ref,
    load_sem,
    all_first,
    all_second,
    all_depth,
    far_total,
    near_total,
    main_far,
    tail,
    side_first,
    side_second,
    side_both,
    charges,
    out_edge,
    out_corner,
    in_edge,
    in_corner,
    grid,
    operand,
    summed,
    lines,
    fine_strips,
    coarse_strips,
    own_coarse,
    out_coarse,
    in_coarse,
    wide_coarse,
    total,
    wide_pot,
    rows_pot,
    send_tail,
    potential,
    upper_first,
    upper_second,
    upper_both,
    read_table,
    send_1,
    recv_1,
    send_2,
    recv_2,
    send_3,
    recv_3,
    send_5,
    recv_5,
):
    here_first = lax.axis_index("gx")
    here_second = lax.axis_index("gy")
    live = count_ref[0, 0]

    def device(a, b):
        return (
            lax.rem(here_first + (a + sizes[0]), sizes[0]),
            lax.rem(here_second + (b + sizes[1]), sizes[1]),
        )

    def send(source, target, out_sem, in_sem, a, b):
        copy = pltpu.make_async_remote_copy(
            src_ref=source,
            dst_ref=target,
            send_sem=out_sem,
            recv_sem=in_sem,
            device_id=device(a, b),
            device_id_type=MESH,
        )
        copy.start()
        return copy

    loads = []
    for at, (source, target) in enumerate(
        [
            (cell_hbm, cell_ref),
            (weight_hbm, weight_ref),
            (charge_hbm, charge_ref),
            (fine_hbm, fine_ref),
            (coarse_hbm, coarse_ref),
        ]
    ):
        load = pltpu.make_async_copy(source, target, load_sem.at[at])
        load.start()
        loads.append(load)

    barrier = pltpu.get_barrier_semaphore()
    for a, b in AROUND:
        pl.semaphore_signal(barrier, inc=1, device_id=device(a, b), device_id_type=MESH)

    for load in loads:
        load.wait()

    far_total[...] = jnp.zeros_like(far_total)
    near_total[...] = jnp.zeros_like(near_total)

    def block_at(step):
        start = pl.multiple_of(step * BLOCK, BLOCK)
        return pl.ds(start, BLOCK), iota((1, BLOCK), 1) + start < live

    def add_rows(sums, parts, depth):
        high, low = split(jnp.concatenate(parts, axis=0))
        both = lax.dot_general(
            jnp.concatenate([high, low], axis=0), depth, LANES_BOTH, preferred_element_type=F32
        )
        sums[...] += both[: high.shape[0]] + both[high.shape[0] :]

    def spread_far(step, carry):
        here, alive = block_at(step)
        weights = weight_ref[:, here].astype(F32)
        rows_first, rows_second, depth = bead_tables(cell_ref[:, here], weights)
        all_first[:, here] = rows_first
        all_second[:, here] = rows_second
        all_depth[:, here] = depth
        rows_first = rows_first * jnp.where(alive, charge_ref[:, here], 0.0)
        parts = [rows_first[x : x + 1] * rows_second[:16] for x in range(16, 19)]
        parts += [rows_second[y : y + 1] * rows_first for y in range(16, 19)]
        parts += [jnp.zeros((8, BLOCK), F32)]
        add_rows(far_total, parts, depth)
        return carry

    def spread_near(step, carry):
        here, alive = block_at(step)
        rows_first = all_first[0:16, here] * jnp.where(alive, charge_ref[:, here], 0.0)
        rows_second = all_second[0:16, here]
        parts = [rows_first[x : x + 1] * rows_second for x in range(16)]
        add_rows(near_total, parts, all_depth[:, here])
        return carry

    steps = charge_ref.shape[1] // BLOCK
    lax.fori_loop(0, steps, spread_far, 0)
    main_far[...] = far_total[0:48].reshape(3, 16, LZ)
    tail[...] = far_total[48:120].reshape(3, 24, LZ)

    pl.semaphore_wait(barrier, 8)

    spills = [
        send(main_far, side_first, send_1.at[0], recv_1.at[0], 1, 0),
        send(tail.at[:, 16:24], side_both, send_1.at[2], recv_1.at[2], 1, 1),
        send(tail.at[:, 0:16], side_second, send_1.at[1], recv_1.at[1], 0, 1),
    ]

    lax.fori_loop(0, steps, spread_near, 0)

    for copy in spills:
        copy.wait()
    charges[...] = near_total[...].reshape(16, 16, LZ)
    charges[0:3] += side_first[...]
    for y in range(3):
        side_second[y, 0:8] += side_both[y]
        charges[:, y, :] += side_second[y]
    grid[8:24, 8:24] = charges[...].astype(BF16).astype(F32)

    out_edge[0] = grid[8:16, 8:24].astype(BF16)
    out_edge[1] = grid[16:24, 8:24].astype(BF16)
    out_edge[2] = grid[8:24, 8:16].reshape(8, 16, LZ).astype(BF16)
    out_edge[3] = grid[8:24, 16:24].reshape(8, 16, LZ).astype(BF16)
    for i in range(2):
        for j in range(2):
            quarter = grid[8 + 8 * i : 16 + 8 * i, 8 + 8 * j : 16 + 8 * j]
            out_corner[2 * i + j] = quarter.reshape(4, 16, LZ).astype(BF16)
    halos = []
    for at, (a, b) in enumerate([(-1, 0), (1, 0), (0, -1), (0, 1)]):
        halos.append(send(out_edge.at[at], in_edge.at[at], send_2.at[at], recv_2.at[at], a, b))
    for at, (a, b) in enumerate([(-1, -1), (-1, 1), (1, -1), (1, 1)]):
        halos.append(
            send(out_corner.at[at], in_corner.at[at], send_2.at[4 + at], recv_2.at[4 + at], a, b)
        )
    lanes = iota((SIDE, LZ), 1)
    taps = iota((SIDE, LZ), 0)
    for at, source in enumerate((fine_ref, coarse_ref)):
        whole = [jnp.zeros((SIDE, LZ), F32)] * 2
        for chunk in range(5):
            placed = jnp.zeros((SIDE, LZ), F32)
            for j in range(4):
                dx = 4 * chunk + j
                if dx < SIDE:
                    place = (lanes == taps + 32 * j).astype(BF16)
                    placed = placed + lax.dot_general(
                        source[dx], place, ROWS_BOTH, preferred_element_type=F32
                    )
            whole.append(placed)
        whole = jnp.concatenate(whole + [jnp.zeros((SIDE, LZ), F32)], axis=1)
        for v in range(4):
            moved = whole if v == 0 else pltpu.roll(whole, STRIP - 32 * v, 1)
            for chunk in range(1, 7):
                lines[at, v, chunk, 0:SIDE] = moved[:, 128 * chunk : 128 * chunk + 128]

    for strips in (fine_strips, coarse_strips):
        strips[:, :, :, 0:128] = jnp.zeros((SIDE, 4, 16, 128), BF16)
        strips[:, :, :, 896:1024] = jnp.zeros((SIDE, 4, 16, 128), BF16)
        strips[:, 0, :, 128:256] = jnp.zeros((SIDE, 16, 128), BF16)
        strips[:, 1:4, :, 768:896] = jnp.zeros((SIDE, 3, 16, 128), BF16)

    def build(dz, carry):
        for at, strips in enumerate((fine_strips, coarse_strips)):
            for v in range(4):
                for chunk in range(2, 7) if v == 0 else range(1, 6):
                    span = slice(128 * chunk, 128 * chunk + 128)
                    line = lines[at, v, chunk, pl.ds(dz, 1)]
                    upper = pltpu.roll(
                        jnp.broadcast_to(line, (8, LZ)), 0, 1, stride=1, stride_axis=0
                    )
                    both = jnp.concatenate([upper, pltpu.roll(upper, 8, 1)], axis=0)
                    strips[dz, v, :, span] = both.astype(BF16)
        return carry

    lax.fori_loop(0, SIDE, build, 0)
    wide_coarse[...] = jnp.zeros_like(wide_coarse)

    for copy in halos:
        copy.wait()
    grid[24:32, 8:24] = in_edge[0].astype(F32)
    grid[0:8, 8:24] = in_edge[1].astype(F32)
    grid[8:24, 24:32] = in_edge[2].astype(F32).reshape(16, 8, LZ)
    grid[8:24, 0:8] = in_edge[3].astype(F32).reshape(16, 8, LZ)
    for i in range(2):
        for j in range(2):
            quarter = in_corner[2 * i + j].astype(F32).reshape(8, 8, LZ)
            grid[24 - 24 * i : 32 - 24 * i, 24 - 24 * j : 32 - 24 * j] = quarter

    gap = (iota((LZ, LZ), 0) - 2 * (iota((LZ, LZ), 1) & 63) + 2) & 127
    spline = jnp.where(gap == 2, 0.75, 0.0)
    spline = jnp.where((gap == 1) | (gap == 3), 0.5, spline)
    spline = jnp.where((gap == 0) | (gap == 4), 0.125, spline).astype(BF16)
    coarse_lines = jnp.dot(
        grid[4:27].reshape(23 * 32, LZ).astype(BF16), spline, preferred_element_type=F32
    ).reshape(23, 32, LZ)
    for i in range(10):
        summed[i] = (
            0.125 * (coarse_lines[2 * i] + coarse_lines[2 * i + 4])
            + 0.5 * (coarse_lines[2 * i + 1] + coarse_lines[2 * i + 3])
            + 0.75 * coarse_lines[2 * i + 2]
        )
    for i in range(10):
        parts = [summed[i, pl.ds(4 + t, 10, stride=2)] for t in range(5)]
        plane = 0.125 * (parts[0] + parts[4]) + 0.5 * (parts[1] + parts[3]) + 0.75 * parts[2]
        own_coarse[i, 0:10] = plane.astype(BF16).astype(F32)
    lower = iota((8, LZ), 1) < 64
    inner = [own_coarse[1 + i, 1:9] for i in range(8)]
    pairs = [jnp.where(lower, inner[2 * j], inner[2 * j + 1]) for j in range(4)]
    mains = [jnp.concatenate(pairs[2 * k : 2 * k + 2], axis=0).astype(BF16) for k in range(2)]
    columns = {1: own_coarse[1:9, 0, :], -1: own_coarse[1:9, 9, :], 0: inner[0]}
    coarse_sends = []
    for at, (a, b) in enumerate(AROUND):
        x = 0 if a > 0 else 9
        y = 0 if b > 0 else 9
        outer = jnp.where(lower, own_coarse[x, 1:9], columns[b])
        corner = jnp.broadcast_to(own_coarse[x, y : y + 1], (8, LZ))
        out_coarse[at, 0] = mains[0]
        out_coarse[at, 1] = mains[1]
        out_coarse[at, 2] = jnp.concatenate([outer, corner], axis=0).astype(BF16)
        coarse_sends.append(
            send(out_coarse.at[at], in_coarse.at[at], send_3.at[at], recv_3.at[at], a, b)
        )
    for i in range(8):
        wide_coarse[9 + i, 9:17] = inner[i]

    def strip_rows(strips, dz):
        columns = []
        for q in range(3):
            blocks = []
            for x in range(8):
                a, v = divmod(8 - x + 8 * q, 4)
                blocks.append(strips[dz, v, :, 128 * a : 128 * a + 256])
            columns.append(jnp.concatenate(blocks, axis=0))
        return jnp.concatenate(columns, axis=1)

    operand[:, 0:LZ] = grid[0:24].reshape(768, LZ).astype(BF16)
    operand[:, LZ:] = grid[8:32].reshape(768, LZ).astype(BF16)
    total[...] = jnp.zeros_like(total)

    def products(strips, right, group):
        rows = jnp.concatenate([strip_rows(strips, dz) for dz in group], axis=0)
        result = jnp.dot(rows, right, preferred_element_type=F32)
        return [result[128 * at : 128 * at + 128] for at in range(len(group))]

    def turned(value, dz):
        return value if dz == 8 else pltpu.roll(value, (136 - dz) % 128, 1)

    def correlate_fine(first, last):
        for start in range(first, last, GROUP):
            group = range(start, min(start + GROUP, last))
            for dz, product in zip(group, products(fine_strips, operand[...], group)):
                total[0] += turned(product[:, :LZ], dz)
                total[1] += turned(product[:, LZ:], dz)

    correlate_fine(0, SIDE)

    for copy in coarse_sends:
        copy.wait()
    for at, (a, b) in enumerate(AROUND):
        x, y = 9 - 8 * a, 9 - 8 * b
        for k in range(2):
            pair_rows = in_coarse[at, k].astype(F32)
            for j in range(2):
                pair = pair_rows[8 * j : 8 * j + 8]
                other = pltpu.roll(pair, 64, 1)
                place = x + 4 * k + 2 * j
                wide_coarse[place, y : y + 8] = jnp.where(lower, pair, other)
                wide_coarse[place + 1, y : y + 8] = jnp.where(lower, other, pair)
        outer_rows = in_coarse[at, 2].astype(F32)
        outer = outer_rows[0:8]
        other = pltpu.roll(outer, 64, 1)
        x_outer = 0 if a > 0 else 25
        y_outer = 0 if b > 0 else 25
        if a != 0:
            wide_coarse[x_outer, y : y + 8] = jnp.where(lower, outer, other)
        if b != 0:
            wide_coarse[x : x + 8, y_outer, :] = jnp.where(lower, other, outer)
        if a != 0 and b != 0:
            wide_coarse[x_outer, y_outer : y_outer + 1] = outer_rows[8:9]
    operand[:, 0:LZ] = wide_coarse[0:24].reshape(768, LZ).astype(BF16)
    operand[:, LZ:] = wide_coarse[8:32].reshape(768, LZ).astype(BF16)
    wide_pot[...] = jnp.zeros_like(wide_pot)

    for start in range(0, SIDE, GROUP):
        group = range(start, min(start + GROUP, SIDE))
        for dz, product in zip(group, products(coarse_strips, operand[...], group)):
            wide_pot[0:8] += turned(product[:, :LZ], dz).reshape(8, 16, LZ)
            wide_pot[8:10] += turned(product[0:32, LZ:], dz).reshape(2, 16, LZ)

    for i in range(8):
        rows_pot[2 * i] = (wide_pot[i] + 6.0 * wide_pot[i + 1] + wide_pot[i + 2]) * 0.125
        rows_pot[2 * i + 1] = (wide_pot[i + 1] + wide_pot[i + 2]) * 0.5
    below = rows_pot[:, 0:8]
    middle = rows_pot[:, 1:9]
    above = rows_pot[:, 2:10]
    even_rows = (below + 6.0 * middle + above) * 0.125
    odd_rows = (middle + above) * 0.5
    for i in range(16):
        potential[i, pl.ds(0, 8, stride=2)] = even_rows[i]
        potential[i, pl.ds(1, 8, stride=2)] = odd_rows[i]
    source = iota((LZ, LZ), 0)
    offset = (iota((LZ, LZ), 1) - 2 * source + 2) & 127
    refine = jnp.where(offset == 2, 0.75, 0.0)
    refine = jnp.where((offset == 1) | (offset == 3), 0.5, refine)
    refine = jnp.where((offset == 0) | (offset == 4), 0.125, refine)
    refine = jnp.where(source < 64, refine, 0.0).astype(BF16)
    high, low = split(potential[...].reshape(256, LZ))
    smooth = jnp.dot(
        jnp.concatenate([high, low], axis=1),
        jnp.concatenate([refine, refine], axis=0),
        preferred_element_type=F32,
    )
    potential[...] = (total[...].reshape(256, LZ) + smooth).reshape(16, 16, LZ)

    for y in range(3):
        send_tail[y] = potential[:, y, :]
    upper = [
        send(potential.at[0:3], upper_first, send_5.at[0], recv_5.at[0], -1, 0),
        send(send_tail.at[:, 0:8], upper_both, send_5.at[2], recv_5.at[2], -1, -1),
        send(send_tail, upper_second, send_5.at[1], recv_5.at[1], 0, -1),
    ]
    grid_ref[...] = potential[...]

    def put_table(start, rows):
        high, low = split(rows)
        read_table[start : start + rows.shape[0], 0:LZ] = high
        read_table[start : start + rows.shape[0], LZ:] = low

    put_table(0, potential[...].reshape(256, LZ))

    def read_near(step, carry):
        here, _ = block_at(step)
        depth = all_depth[:, here]
        along = jnp.dot(
            read_table[0:256], jnp.concatenate([depth, depth], axis=0), preferred_element_type=F32
        )
        rows_first = all_first[:, here]
        near = jnp.zeros((16, BLOCK), F32)
        for x in range(16):
            near = near + rows_first[x : x + 1] * along[16 * x : 16 * x + 16]
        near = near * all_second[0:16, here]
        bead_ref[:, here] = jnp.sum(near[:8] + near[8:], axis=0, keepdims=True)
        return carry

    lax.fori_loop(0, steps, read_near, 0)

    for copy in upper:
        copy.wait()
    put_table(256, upper_first[...].reshape(48, LZ))
    ends = []
    for y in range(3):
        ends += [upper_second[y], upper_both[y]]
    ends += [jnp.zeros((8, LZ), F32)]
    put_table(304, jnp.concatenate(ends, axis=0))

    def read_far(step, carry):
        here, alive = block_at(step)
        depth = all_depth[:, here]
        along = jnp.dot(
            read_table[256:384],
            jnp.concatenate([depth, depth], axis=0),
            preferred_element_type=F32,
        )
        rows_first = all_first[:, here]
        rows_second = all_second[:, here]
        near = jnp.zeros((16, BLOCK), F32)
        for x in range(3):
            near = near + rows_first[16 + x : 17 + x] * along[16 * x : 16 * x + 16]
        far = jnp.zeros((24, BLOCK), F32)
        for y in range(3):
            far = far + rows_second[16 + y : 17 + y] * along[48 + 24 * y : 72 + 24 * y]
        near = near * rows_second[:16]
        far = far * rows_first
        both = near[:8] + near[8:] + far[:8] + far[8:16] + far[16:]
        value = bead_ref[:, here] + jnp.sum(both, axis=0, keepdims=True)
        bead_ref[:, here] = jnp.where(alive, value, 0.0)
        return carry

    lax.fori_loop(0, steps, read_far, 0)


def hand_over(bead_from, grid_from, bead_to, grid_to):
    bead_to[...] = bead_from[...]
    grid_to[...] = grid_from[...]


def on_device(sizes, bead_charge, bead_cell, bead_count, interp_weights, kernel_fine, kernel_coarse):
    slots = bead_charge.shape[-1]
    charge = bead_charge.reshape(1, slots)
    cells = bead_cell.reshape(1, slots)
    weights = interp_weights.reshape(12, slots)
    vmem = pl.BlockSpec(memory_space=pltpu.VMEM)
    smem = pl.BlockSpec(memory_space=pltpu.SMEM)
    anywhere = pl.BlockSpec(memory_space=pl.ANY)
    dma = pltpu.SemaphoreType.DMA
    scratch = [
        pltpu.VMEM((1, slots), F32),
        pltpu.VMEM((1, slots), jnp.int32),
        pltpu.VMEM((12, slots), BF16),
        pltpu.VMEM((SIDE, SIDE, SIDE), BF16),
        pltpu.VMEM((SIDE, SIDE, SIDE), BF16),
        dma((5,)),
        pltpu.VMEM((24, slots), F32),
        pltpu.VMEM((24, slots), F32),
        pltpu.VMEM((LZ, slots), BF16),
        pltpu.VMEM((128, LZ), F32),
        pltpu.VMEM((256, LZ), F32),
        pltpu.VMEM((3, 16, LZ), F32),
        pltpu.VMEM((3, 24, LZ), F32),
        pltpu.VMEM((3, 16, LZ), F32),
        pltpu.VMEM((3, 16, LZ), F32),
        pltpu.VMEM((3, 8, LZ), F32),
        pltpu.VMEM((16, 16, LZ), F32),
        pltpu.VMEM((4, 8, 16, LZ), BF16),
        pltpu.VMEM((4, 4, 16, LZ), BF16),
        pltpu.VMEM((4, 8, 16, LZ), BF16),
        pltpu.VMEM((4, 4, 16, LZ), BF16),
        pltpu.VMEM((32, 32, LZ), F32),
        pltpu.VMEM((768, 2 * LZ), BF16),
        pltpu.VMEM((10, 32, LZ), F32),
        pltpu.VMEM((2, 4, 8, 24, LZ), F32),
        pltpu.VMEM((SIDE, 4, 16, STRIP), BF16),
        pltpu.VMEM((SIDE, 4, 16, STRIP), BF16),
        pltpu.VMEM((10, 16, LZ), F32),
        pltpu.VMEM((8, 3, 16, LZ), BF16),
        pltpu.VMEM((8, 3, 16, LZ), BF16),
        pltpu.VMEM((32, 32, LZ), F32),
        pltpu.VMEM((2, LZ, LZ), F32),
        pltpu.VMEM((10, 16, LZ), F32),
        pltpu.VMEM((16, 16, LZ), F32),
        pltpu.VMEM((3, 16, LZ), F32),
        pltpu.VMEM((16, 16, LZ), F32),
        pltpu.VMEM((3, 16, LZ), F32),
        pltpu.VMEM((3, 16, LZ), F32),
        pltpu.VMEM((3, 8, LZ), F32),
        pltpu.VMEM((ROWS, 2 * LZ), BF16),
    ]
    for count in (3, 8, 8, 3):
        scratch += [dma((count,)), dma((count,))]
    bead, grid = pl.pallas_call(
        functools.partial(melt_kernel, sizes),
        out_shape=(
            jax.ShapeDtypeStruct((1, slots), F32),
            jax.ShapeDtypeStruct((16, 16, LZ), F32),
        ),
        in_specs=[smem] + [anywhere] * 5,
        out_specs=(vmem, vmem),
        scratch_shapes=scratch,
        compiler_params=pltpu.CompilerParams(
            collective_id=0, has_side_effects=True, vmem_limit_bytes=60 << 20
        ),
        name="melt",
    )(bead_count, charge, cells, weights, kernel_fine, kernel_coarse)
    bead, grid = pl.pallas_call(
        hand_over,
        out_shape=(
            jax.ShapeDtypeStruct((1, slots), F32),
            jax.ShapeDtypeStruct((16, 16, LZ), F32),
        ),
        in_specs=[vmem, vmem],
        out_specs=(vmem, vmem),
        name="hand_over",
    )(bead, grid)
    return (bead.reshape(1, 1, slots), grid)


def solution(mesh):
    sizes = (mesh.shape["gx"], mesh.shape["gy"])
    return jax.shard_map(
        functools.partial(on_device, sizes),
        mesh=mesh,
        in_specs=(
            P("gx", "gy", None),
            P("gx", "gy", None),
            P("gx", "gy"),
            P("gx", "gy", None, None),
            P(),
            P(),
        ),
        out_specs=(P("gx", "gy", None), P("gx", "gy", None)),
        check_vma=False,
    )
```

```python
import functools

import jax
import jax.numpy as jnp
from jax import lax
from jax.experimental import pallas as pl
from jax.experimental.pallas import tpu as pltpu
from jax.sharding import PartitionSpec as P

LX = 16
LY = 16
LZ = 128
SIDE = 17
BLOCK = 8192
READ_BLOCK = 16384
ROWS = 384
STRIP = 1024
GROUP = 5
MESH = pl.DeviceIdType.MESH
F32 = jnp.float32
BF16 = jnp.bfloat16
LANES_BOTH = (((1,), (1,)), ((), ()))
ROWS_BOTH = (((0,), (0,)), ((), ()))
AROUND = [(a, b) for a in (-1, 1, 0) for b in (0, -1, 1) if (a, b) != (0, 0)]


def iota(shape, dim):
    return lax.broadcasted_iota(jnp.int32, shape, dim)


def split(value):
    high = value.astype(BF16)
    low = (value - high.astype(F32)).astype(BF16)
    return high, low


def bead_tables(cells, weights):
    count = cells.shape[1]
    first = cells >> 11
    second = (cells >> 7) & 15
    third = cells & 127
    rows = iota((24, count), 0)
    away_first = rows - first
    away_second = rows - second
    rows_first = jnp.zeros((24, count), F32)
    rows_second = jnp.zeros((24, count), F32)
    for tap in range(4):
        rows_first = jnp.where(away_first == tap, weights[tap : tap + 1], rows_first)
        rows_second = jnp.where(away_second == tap, weights[4 + tap : 5 + tap], rows_second)
    depth = jnp.zeros((LZ, count), BF16)
    places = iota((LZ, count), 0).astype(F32).astype(BF16)
    for tap in range(4):
        target = ((third + tap) & 127).astype(F32).astype(BF16)
        depth = jnp.where(places == target, weights[8 + tap : 9 + tap].astype(BF16), depth)
    return rows_first, rows_second, depth


def melt_kernel(
    sizes,
    count_ref,
    charge_hbm,
    cell_hbm,
    weight_hbm,
    fine_hbm,
    coarse_hbm,
    bead_ref,
    grid_ref,
    charge_ref,
    cell_ref,
    weight_ref,
    fine_ref,
    coarse_ref,
    load_sem,
    all_first,
    all_second,
    all_depth,
    far_total,
    near_total,
    main_far,
    tail,
    side_first,
    side_second,
    side_both,
    beside,
    beyond,
    low_edge,
    low_corner,
    charges,
    out_edge,
    out_corner,
    in_edge,
    in_corner,
    grid,
    operand,
    summed,
    lines,
    fine_strips,
    coarse_strips,
    own_coarse,
    out_coarse,
    in_coarse,
    wide_coarse,
    total,
    wide_pot,
    rows_pot,
    send_tail,
    potential,
    upper_first,
    upper_second,
    upper_both,
    read_table,
    send_1,
    recv_1,
    send_2,
    recv_2,
    send_3,
    recv_3,
    send_5,
    recv_5,
):
    here_first = lax.axis_index("gx")
    here_second = lax.axis_index("gy")
    live = count_ref[0, 0]

    def device(a, b):
        return (
            lax.rem(here_first + (a + sizes[0]), sizes[0]),
            lax.rem(here_second + (b + sizes[1]), sizes[1]),
        )

    def send(source, target, out_sem, in_sem, a, b):
        copy = pltpu.make_async_remote_copy(
            src_ref=source,
            dst_ref=target,
            send_sem=out_sem,
            recv_sem=in_sem,
            device_id=device(a, b),
            device_id_type=MESH,
        )
        copy.start()
        return copy

    loads = []
    for at, (source, target) in enumerate(
        [
            (cell_hbm, cell_ref),
            (weight_hbm, weight_ref),
            (charge_hbm, charge_ref),
            (fine_hbm, fine_ref),
            (coarse_hbm, coarse_ref),
        ]
    ):
        load = pltpu.make_async_copy(source, target, load_sem.at[at])
        load.start()
        loads.append(load)

    barrier = pltpu.get_barrier_semaphore()
    for a, b in AROUND:
        pl.semaphore_signal(barrier, inc=1, device_id=device(a, b), device_id_type=MESH)

    for load in loads:
        load.wait()

    far_total[...] = jnp.zeros_like(far_total)
    near_total[...] = jnp.zeros_like(near_total)

    def block_at(step, size):
        start = pl.multiple_of(step * size, size)
        return pl.ds(start, size), iota((1, size), 1) + start < live

    def add_rows(sums, parts, depth):
        high, low = split(jnp.concatenate(parts, axis=0))
        both = lax.dot_general(
            jnp.concatenate([high, low], axis=0), depth, LANES_BOTH, preferred_element_type=F32
        )
        sums[...] += both[: high.shape[0]] + both[high.shape[0] :]

    def spread_far(step, carry):
        here, alive = block_at(step, BLOCK)
        weights = weight_ref[:, here].astype(F32)
        rows_first, rows_second, depth = bead_tables(cell_ref[:, here], weights)
        all_first[:, here] = rows_first
        all_second[:, here] = rows_second
        all_depth[:, here] = depth
        rows_first = rows_first * jnp.where(alive, charge_ref[:, here], 0.0)
        parts = [rows_first[x : x + 1] * rows_second[:16] for x in range(16, 19)]
        parts += [rows_second[y : y + 1] * rows_first for y in range(16, 19)]
        parts += [jnp.zeros((8, BLOCK), F32)]
        add_rows(far_total, parts, depth)
        return carry

    def spread_near(step, carry):
        here, alive = block_at(step, BLOCK)
        rows_first = all_first[0:16, here] * jnp.where(alive, charge_ref[:, here], 0.0)
        rows_second = all_second[0:16, here]
        parts = [rows_first[x : x + 1] * rows_second for x in range(16)]
        add_rows(near_total, parts, all_depth[:, here])
        return carry

    steps = charge_ref.shape[1] // BLOCK
    lax.fori_loop(0, steps, spread_far, 0)
    main_far[...] = far_total[0:48].reshape(3, 16, LZ)
    tail[...] = far_total[48:120].reshape(3, 24, LZ)

    pl.semaphore_wait(barrier, 8)

    spills_first = [
        send(main_far, side_first, send_1.at[0], recv_1.at[0], 1, 0),
        send(tail.at[:, 16:24], side_both, send_1.at[1], recv_1.at[1], 1, 1),
    ]
    spills_second = [
        send(tail, side_second, send_1.at[2], recv_1.at[2], 0, 1),
        send(main_far.at[:, 8:16], beside.at[0], send_1.at[3], recv_1.at[3], 0, 1),
        send(main_far.at[:, 0:8], beside.at[1], send_1.at[4], recv_1.at[4], 0, -1),
    ]

    lax.fori_loop(0, steps, spread_near, 0)

    for copy in spills_second:
        copy.wait()
    charges[...] = near_total[...].reshape(16, 16, LZ)
    beyond[:, 0:8] = beside[0]
    beyond[:, 8:24] = main_far[...]
    beyond[:, 24:32] = beside[1]
    for y in range(3):
        charges[:, y, :] += side_second[y, 0:16]
        beyond[:, 8 + y, :] += side_second[y, 16:19]
        beyond[:, 24 + y, :] += tail[y, 16:19]
    grid[8:24, 8:24] = charges[...].astype(BF16).astype(F32)

    out_edge[0, 3:8] = grid[11:16, 8:24].astype(BF16)
    out_edge[1] = grid[16:24, 8:24].astype(BF16)
    for i in range(2):
        for j in range(2):
            quarter = grid[8 + 8 * i : 16 + 8 * i, 8 + 8 * j : 16 + 8 * j]
            out_corner[2 * i + j] = quarter.reshape(4, 16, LZ).astype(BF16)
    halos = []
    for at, (source, target, a, b) in enumerate(
        [
            (charges.at[0:3], low_edge, -1, 0),
            (out_edge.at[1], in_edge.at[1], 1, 0),
            (out_edge.at[0, 3:8], in_edge.at[0, 3:8], -1, 0),
            (charges.at[0:3, 0:8], low_corner.at[0], -1, -1),
            (charges.at[0:3, 8:16], low_corner.at[1], -1, 1),
            (out_corner.at[2], in_corner.at[2], 1, -1),
            (out_corner.at[3], in_corner.at[3], 1, 1),
            (out_corner.at[0, 1:4], in_corner.at[0, 1:4], -1, -1),
            (out_corner.at[1, 1:4], in_corner.at[1, 1:4], -1, 1),
        ]
    ):
        halos.append(send(source, target, send_2.at[at], recv_2.at[at], a, b))

    lanes = iota((SIDE, LZ), 1)
    taps = iota((SIDE, LZ), 0)
    for at, source in enumerate((fine_ref, coarse_ref)):
        whole = [jnp.zeros((SIDE, LZ), F32)] * 2
        for chunk in range(5):
            placed = jnp.zeros((SIDE, LZ), F32)
            for j in range(4):
                dx = 4 * chunk + j
                if dx < SIDE:
                    place = (lanes == taps + 32 * j).astype(BF16)
                    placed = placed + lax.dot_general(
                        source[dx], place, ROWS_BOTH, preferred_element_type=F32
                    )
            whole.append(placed)
        whole = jnp.concatenate(whole + [jnp.zeros((SIDE, LZ), F32)], axis=1)
        for v in range(4):
            moved = whole if v == 0 else pltpu.roll(whole, STRIP - 32 * v, 1)
            for chunk in range(1, 7):
                lines[at, v, chunk, 0:SIDE] = moved[:, 128 * chunk : 128 * chunk + 128]

    for strips in (fine_strips, coarse_strips):
        strips[:, :, :, 0:128] = jnp.zeros((SIDE, 4, 16, 128), BF16)
        strips[:, :, :, 896:1024] = jnp.zeros((SIDE, 4, 16, 128), BF16)
        strips[:, 0, :, 128:256] = jnp.zeros((SIDE, 16, 128), BF16)
        strips[:, 1:4, :, 768:896] = jnp.zeros((SIDE, 3, 16, 128), BF16)

    def build(dz, carry):
        for at, strips in enumerate((fine_strips, coarse_strips)):
            for v in range(4):
                for chunk in range(2, 7) if v == 0 else range(1, 6):
                    span = slice(128 * chunk, 128 * chunk + 128)
                    line = lines[at, v, chunk, pl.ds(dz, 1)]
                    upper = pltpu.roll(
                        jnp.broadcast_to(line, (8, LZ)), 0, 1, stride=1, stride_axis=0
                    )
                    both = jnp.concatenate([upper, pltpu.roll(upper, 8, 1)], axis=0)
                    strips[dz, v, :, span] = both.astype(BF16)
        return carry

    lax.fori_loop(0, SIDE, build, 0)
    wide_coarse[...] = jnp.zeros_like(wide_coarse)

    for copy in spills_first:
        copy.wait()
    for y in range(3):
        side_first[:, y, :] += side_both[y, 0:3]
    grid[8:11, 8:24] = (charges[0:3] + side_first[...]).astype(BF16).astype(F32)
    out_edge[2] = grid[8:24, 8:16].reshape(8, 16, LZ).astype(BF16)
    out_edge[3] = grid[8:24, 16:24].reshape(8, 16, LZ).astype(BF16)
    for at, b in ((2, -1), (3, 1)):
        halos.append(
            send(out_edge.at[at], in_edge.at[at], send_2.at[7 + at], recv_2.at[7 + at], 0, b)
        )
    for copy in halos:
        copy.wait()
    grid[27:32, 8:24] = in_edge[0, 3:8].astype(F32)
    grid[24:27, 8:24] = (low_edge[...] + beyond[:, 8:24]).astype(BF16).astype(F32)
    grid[24:27, 24:32] = (low_corner[0] + beyond[:, 24:32]).astype(BF16).astype(F32)
    grid[24:27, 0:8] = (low_corner[1] + beyond[:, 0:8]).astype(BF16).astype(F32)
    grid[0:8, 8:24] = in_edge[1].astype(F32)
    grid[8:24, 24:32] = in_edge[2].astype(F32).reshape(16, 8, LZ)
    grid[8:24, 0:8] = in_edge[3].astype(F32).reshape(16, 8, LZ)
    for j in range(2):
        y = 24 - 24 * j
        upper_quarter = in_corner[j, 1:4].astype(F32).reshape(6, 8, LZ)
        grid[27:32, y : y + 8] = upper_quarter[1:6]
        grid[0:8, y : y + 8] = in_corner[2 + j].astype(F32).reshape(8, 8, LZ)

    gap = (iota((LZ, LZ), 0) - 2 * (iota((LZ, LZ), 1) & 63) + 2) & 127
    spline = jnp.where(gap == 2, 0.75, 0.0)
    spline = jnp.where((gap == 1) | (gap == 3), 0.5, spline)
    spline = jnp.where((gap == 0) | (gap == 4), 0.125, spline).astype(BF16)
    coarse_lines = jnp.dot(
        grid[4:27].reshape(23 * 32, LZ).astype(BF16), spline, preferred_element_type=F32
    ).reshape(23, 32, LZ)
    for i in range(10):
        summed[i] = (
            0.125 * (coarse_lines[2 * i] + coarse_lines[2 * i + 4])
            + 0.5 * (coarse_lines[2 * i + 1] + coarse_lines[2 * i + 3])
            + 0.75 * coarse_lines[2 * i + 2]
        )
    for i in range(10):
        parts = [summed[i, pl.ds(4 + t, 10, stride=2)] for t in range(5)]
        plane = 0.125 * (parts[0] + parts[4]) + 0.5 * (parts[1] + parts[3]) + 0.75 * parts[2]
        own_coarse[i, 0:10] = plane.astype(BF16).astype(F32)
    lower = iota((8, LZ), 1) < 64
    inner = [own_coarse[1 + i, 1:9] for i in range(8)]
    pairs = [jnp.where(lower, inner[2 * j], inner[2 * j + 1]) for j in range(4)]
    mains = [jnp.concatenate(pairs[2 * k : 2 * k + 2], axis=0).astype(BF16) for k in range(2)]
    columns = {1: own_coarse[1:9, 0, :], -1: own_coarse[1:9, 9, :], 0: inner[0]}
    coarse_sends = []
    for at, (a, b) in enumerate(AROUND):
        x = 0 if a > 0 else 9
        y = 0 if b > 0 else 9
        outer = jnp.where(lower, own_coarse[x, 1:9], columns[b])
        corner = jnp.broadcast_to(own_coarse[x, y : y + 1], (8, LZ))
        out_coarse[at, 0] = mains[0]
        out_coarse[at, 1] = mains[1]
        out_coarse[at, 2] = jnp.concatenate([outer, corner], axis=0).astype(BF16)
        coarse_sends.append(
            send(out_coarse.at[at], in_coarse.at[at], send_3.at[at], recv_3.at[at], a, b)
        )
    for i in range(8):
        wide_coarse[9 + i, 9:17] = inner[i]

    def strip_rows(strips, dz):
        columns = []
        for q in range(3):
            blocks = []
            for x in range(8):
                a, v = divmod(8 - x + 8 * q, 4)
                blocks.append(strips[dz, v, :, 128 * a : 128 * a + 256])
            columns.append(jnp.concatenate(blocks, axis=0))
        return jnp.concatenate(columns, axis=1)

    operand[:, 0:LZ] = grid[0:24].reshape(768, LZ).astype(BF16)
    operand[:, LZ:] = grid[8:32].reshape(768, LZ).astype(BF16)
    total[...] = jnp.zeros_like(total)

    def products(strips, right, group):
        rows = jnp.concatenate([strip_rows(strips, dz) for dz in group], axis=0)
        result = jnp.dot(rows, right, preferred_element_type=F32)
        return [result[128 * at : 128 * at + 128] for at in range(len(group))]

    def turned(value, dz):
        return value if dz == 8 else pltpu.roll(value, (136 - dz) % 128, 1)

    def correlate_fine(first, last):
        for start in range(first, last, GROUP):
            group = range(start, min(start + GROUP, last))
            for dz, product in zip(group, products(fine_strips, operand[...], group)):
                total[0] += turned(product[:, :LZ], dz)
                total[1] += turned(product[:, LZ:], dz)

    correlate_fine(0, SIDE)

    for copy in coarse_sends:
        copy.wait()
    for at, (a, b) in enumerate(AROUND):
        x, y = 9 - 8 * a, 9 - 8 * b
        for k in range(2):
            pair_rows = in_coarse[at, k].astype(F32)
            for j in range(2):
                pair = pair_rows[8 * j : 8 * j + 8]
                other = pltpu.roll(pair, 64, 1)
                place = x + 4 * k + 2 * j
                wide_coarse[place, y : y + 8] = jnp.where(lower, pair, other)
                wide_coarse[place + 1, y : y + 8] = jnp.where(lower, other, pair)
        outer_rows = in_coarse[at, 2].astype(F32)
        outer = outer_rows[0:8]
        other = pltpu.roll(outer, 64, 1)
        x_outer = 0 if a > 0 else 25
        y_outer = 0 if b > 0 else 25
        if a != 0:
            wide_coarse[x_outer, y : y + 8] = jnp.where(lower, outer, other)
        if b != 0:
            wide_coarse[x : x + 8, y_outer, :] = jnp.where(lower, other, outer)
        if a != 0 and b != 0:
            wide_coarse[x_outer, y_outer : y_outer + 1] = outer_rows[8:9]
    operand[:, 0:LZ] = wide_coarse[0:24].reshape(768, LZ).astype(BF16)
    operand[:, LZ:] = wide_coarse[8:32].reshape(768, LZ).astype(BF16)
    wide_pot[...] = jnp.zeros_like(wide_pot)

    for start in range(0, SIDE, GROUP):
        group = range(start, min(start + GROUP, SIDE))
        for dz, product in zip(group, products(coarse_strips, operand[...], group)):
            wide_pot[0:8] += turned(product[:, :LZ], dz).reshape(8, 16, LZ)
            wide_pot[8:10] += turned(product[0:32, LZ:], dz).reshape(2, 16, LZ)

    for i in range(8):
        rows_pot[2 * i] = (wide_pot[i] + 6.0 * wide_pot[i + 1] + wide_pot[i + 2]) * 0.125
        rows_pot[2 * i + 1] = (wide_pot[i + 1] + wide_pot[i + 2]) * 0.5
    below = rows_pot[:, 0:8]
    middle = rows_pot[:, 1:9]
    above = rows_pot[:, 2:10]
    even_rows = (below + 6.0 * middle + above) * 0.125
    odd_rows = (middle + above) * 0.5
    for i in range(16):
        potential[i, pl.ds(0, 8, stride=2)] = even_rows[i]
        potential[i, pl.ds(1, 8, stride=2)] = odd_rows[i]
    source = iota((LZ, LZ), 0)
    offset = (iota((LZ, LZ), 1) - 2 * source + 2) & 127
    refine = jnp.where(offset == 2, 0.75, 0.0)
    refine = jnp.where((offset == 1) | (offset == 3), 0.5, refine)
    refine = jnp.where((offset == 0) | (offset == 4), 0.125, refine)
    refine = jnp.where(source < 64, refine, 0.0).astype(BF16)
    high, low = split(potential[...].reshape(256, LZ))
    smooth = jnp.dot(
        jnp.concatenate([high, low], axis=1),
        jnp.concatenate([refine, refine], axis=0),
        preferred_element_type=F32,
    )
    potential[...] = (total[...].reshape(256, LZ) + smooth).reshape(16, 16, LZ)

    for y in range(3):
        send_tail[y] = potential[:, y, :]
    upper = [
        send(potential.at[0:3], upper_first, send_5.at[0], recv_5.at[0], -1, 0),
        send(send_tail.at[:, 0:8], upper_both, send_5.at[2], recv_5.at[2], -1, -1),
        send(send_tail, upper_second, send_5.at[1], recv_5.at[1], 0, -1),
    ]
    grid_ref[...] = potential[...]

    def put_table(start, rows):
        high, low = split(rows)
        read_table[start : start + rows.shape[0], 0:LZ] = high
        read_table[start : start + rows.shape[0], LZ:] = low

    put_table(0, potential[...].reshape(256, LZ))

    slots = charge_ref.shape[1]

    def read_near(step, carry):
        here, _ = block_at(step, READ_BLOCK)
        depth = all_depth[:, here]
        along = jnp.dot(
            read_table[0:256], jnp.concatenate([depth, depth], axis=0), preferred_element_type=F32
        )
        rows_first = all_first[:, here]
        near = jnp.zeros((16, READ_BLOCK), F32)
        for x in range(16):
            near = near + rows_first[x : x + 1] * along[16 * x : 16 * x + 16]
        near = near * all_second[0:16, here]
        bead_ref[:, here] = jnp.sum(near[:8] + near[8:], axis=0, keepdims=True)
        return carry

    lax.fori_loop(0, slots // READ_BLOCK, read_near, 0)

    for copy in upper:
        copy.wait()
    put_table(256, upper_first[...].reshape(48, LZ))
    ends = []
    for y in range(3):
        ends += [upper_second[y], upper_both[y]]
    ends += [jnp.zeros((8, LZ), F32)]
    put_table(304, jnp.concatenate(ends, axis=0))

    def read_far(step, carry):
        here, alive = block_at(step, READ_BLOCK)
        depth = all_depth[:, here]
        along = jnp.dot(
            read_table[256:384],
            jnp.concatenate([depth, depth], axis=0),
            preferred_element_type=F32,
        )
        rows_first = all_first[:, here]
        rows_second = all_second[:, here]
        near = jnp.zeros((16, READ_BLOCK), F32)
        for x in range(3):
            near = near + rows_first[16 + x : 17 + x] * along[16 * x : 16 * x + 16]
        far = jnp.zeros((24, READ_BLOCK), F32)
        for y in range(3):
            far = far + rows_second[16 + y : 17 + y] * along[48 + 24 * y : 72 + 24 * y]
        near = near * rows_second[:16]
        far = far * rows_first
        both = near[:8] + near[8:] + far[:8] + far[8:16] + far[16:]
        value = bead_ref[:, here] + jnp.sum(both, axis=0, keepdims=True)
        bead_ref[:, here] = jnp.where(alive, value, 0.0)
        return carry

    lax.fori_loop(0, slots // READ_BLOCK, read_far, 0)


def hand_over(bead_from, grid_from, bead_to, grid_to):
    bead_to[...] = bead_from[...]
    grid_to[...] = grid_from[...]


def on_device(sizes, bead_charge, bead_cell, bead_count, interp_weights, kernel_fine, kernel_coarse):
    slots = bead_charge.shape[-1]
    charge = bead_charge.reshape(1, slots)
    cells = bead_cell.reshape(1, slots)
    weights = interp_weights.reshape(12, slots)
    vmem = pl.BlockSpec(memory_space=pltpu.VMEM)
    smem = pl.BlockSpec(memory_space=pltpu.SMEM)
    anywhere = pl.BlockSpec(memory_space=pl.ANY)
    dma = pltpu.SemaphoreType.DMA
    scratch = [
        pltpu.VMEM((1, slots), F32),
        pltpu.VMEM((1, slots), jnp.int32),
        pltpu.VMEM((12, slots), BF16),
        pltpu.VMEM((SIDE, SIDE, SIDE), BF16),
        pltpu.VMEM((SIDE, SIDE, SIDE), BF16),
        dma((5,)),
        pltpu.VMEM((24, slots), F32),
        pltpu.VMEM((24, slots), F32),
        pltpu.VMEM((LZ, slots), BF16),
        pltpu.VMEM((128, LZ), F32),
        pltpu.VMEM((256, LZ), F32),
        pltpu.VMEM((3, 16, LZ), F32),
        pltpu.VMEM((3, 24, LZ), F32),
        pltpu.VMEM((3, 16, LZ), F32),
        pltpu.VMEM((3, 24, LZ), F32),
        pltpu.VMEM((3, 8, LZ), F32),
        pltpu.VMEM((2, 3, 8, LZ), F32),
        pltpu.VMEM((3, 32, LZ), F32),
        pltpu.VMEM((3, 16, LZ), F32),
        pltpu.VMEM((2, 3, 8, LZ), F32),
        pltpu.VMEM((16, 16, LZ), F32),
        pltpu.VMEM((4, 8, 16, LZ), BF16),
        pltpu.VMEM((4, 4, 16, LZ), BF16),
        pltpu.VMEM((4, 8, 16, LZ), BF16),
        pltpu.VMEM((4, 4, 16, LZ), BF16),
        pltpu.VMEM((32, 32, LZ), F32),
        pltpu.VMEM((768, 2 * LZ), BF16),
        pltpu.VMEM((10, 32, LZ), F32),
        pltpu.VMEM((2, 4, 8, 24, LZ), F32),
        pltpu.VMEM((SIDE, 4, 16, STRIP), BF16),
        pltpu.VMEM((SIDE, 4, 16, STRIP), BF16),
        pltpu.VMEM((10, 16, LZ), F32),
        pltpu.VMEM((8, 3, 16, LZ), BF16),
        pltpu.VMEM((8, 3, 16, LZ), BF16),
        pltpu.VMEM((32, 32, LZ), F32),
        pltpu.VMEM((2, LZ, LZ), F32),
        pltpu.VMEM((10, 16, LZ), F32),
        pltpu.VMEM((16, 16, LZ), F32),
        pltpu.VMEM((3, 16, LZ), F32),
        pltpu.VMEM((16, 16, LZ), F32),
        pltpu.VMEM((3, 16, LZ), F32),
        pltpu.VMEM((3, 16, LZ), F32),
        pltpu.VMEM((3, 8, LZ), F32),
        pltpu.VMEM((ROWS, 2 * LZ), BF16),
    ]
    for count in (5, 11, 8, 3):
        scratch += [dma((count,)), dma((count,))]
    bead, grid = pl.pallas_call(
        functools.partial(melt_kernel, sizes),
        out_shape=(
            jax.ShapeDtypeStruct((1, slots), F32),
            jax.ShapeDtypeStruct((16, 16, LZ), F32),
        ),
        in_specs=[smem] + [anywhere] * 5,
        out_specs=(vmem, vmem),
        scratch_shapes=scratch,
        compiler_params=pltpu.CompilerParams(
            collective_id=0, has_side_effects=True, vmem_limit_bytes=60 << 20
        ),
        name="melt",
    )(bead_count, charge, cells, weights, kernel_fine, kernel_coarse)
    bead, grid = pl.pallas_call(
        hand_over,
        out_shape=(
            jax.ShapeDtypeStruct((1, slots), F32),
            jax.ShapeDtypeStruct((16, 16, LZ), F32),
        ),
        in_specs=[vmem, vmem],
        out_specs=(vmem, vmem),
        name="hand_over",
    )(bead, grid)
    return (bead.reshape(1, 1, slots), grid)


def solution(mesh):
    sizes = (mesh.shape["gx"], mesh.shape["gy"])
    return jax.shard_map(
        functools.partial(on_device, sizes),
        mesh=mesh,
        in_specs=(
            P("gx", "gy", None),
            P("gx", "gy", None),
            P("gx", "gy"),
            P("gx", "gy", None, None),
            P(),
            P(),
        ),
        out_specs=(P("gx", "gy", None), P("gx", "gy", None)),
        check_vma=False,
    )
```

```python
import functools

import jax
import jax.numpy as jnp
from jax import lax
from jax.experimental import pallas as pl
from jax.experimental.pallas import tpu as pltpu
from jax.sharding import PartitionSpec as P

LX = 16
LY = 16
LZ = 128
SIDE = 17
FAR_BLOCK = 16384
NEAR_BLOCK = 16384
READ_BLOCK = 16384
ROWS = 384
STRIP = 1024
GROUP = 9
MESH = pl.DeviceIdType.MESH
F32 = jnp.float32
BF16 = jnp.bfloat16
LANES_BOTH = (((1,), (1,)), ((), ()))
ROWS_BOTH = (((0,), (0,)), ((), ()))
AROUND = [(a, b) for a in (-1, 1, 0) for b in (0, -1, 1) if (a, b) != (0, 0)]


def iota(shape, dim):
    return lax.broadcasted_iota(jnp.int32, shape, dim)


def split(value):
    high = value.astype(BF16)
    low = (value - high.astype(F32)).astype(BF16)
    return high, low


def bead_tables(cells, weights):
    count = cells.shape[1]
    first = cells >> 11
    second = (cells >> 7) & 15
    third = cells & 127
    rows = iota((24, count), 0)
    away_first = rows - first
    away_second = rows - second
    rows_first = jnp.zeros((24, count), F32)
    rows_second = jnp.zeros((24, count), F32)
    for tap in range(4):
        rows_first = jnp.where(away_first == tap, weights[tap : tap + 1], rows_first)
        rows_second = jnp.where(away_second == tap, weights[4 + tap : 5 + tap], rows_second)
    depth = jnp.zeros((LZ, count), BF16)
    places = iota((LZ, count), 0).astype(F32).astype(BF16)
    for tap in range(4):
        target = ((third + tap) & 127).astype(F32).astype(BF16)
        depth = jnp.where(places == target, weights[8 + tap : 9 + tap].astype(BF16), depth)
    return rows_first, rows_second, depth


def melt_kernel(
    sizes,
    count_ref,
    charge_hbm,
    cell_hbm,
    weight_hbm,
    fine_hbm,
    coarse_hbm,
    bead_ref,
    grid_ref,
    charge_ref,
    cell_ref,
    weight_ref,
    fine_ref,
    coarse_ref,
    load_sem,
    all_first,
    all_second,
    all_depth,
    far_total,
    near_total,
    main_far,
    tail,
    side_first,
    side_second,
    side_both,
    beside,
    beyond,
    low_edge,
    low_corner,
    charges,
    out_edge,
    out_corner,
    in_edge,
    in_corner,
    grid,
    operand,
    summed,
    lines,
    fine_strips,
    coarse_strips,
    own_coarse,
    out_coarse,
    in_coarse,
    wide_coarse,
    total,
    wide_pot,
    rows_pot,
    send_tail,
    potential,
    upper_first,
    upper_second,
    upper_both,
    read_table,
    send_1,
    recv_1,
    send_2,
    recv_2,
    send_3,
    recv_3,
    send_5,
    recv_5,
):
    here_first = lax.axis_index("gx")
    here_second = lax.axis_index("gy")
    live = count_ref[0, 0]

    def device(a, b):
        return (
            lax.rem(here_first + (a + sizes[0]), sizes[0]),
            lax.rem(here_second + (b + sizes[1]), sizes[1]),
        )

    def send(source, target, out_sem, in_sem, a, b):
        copy = pltpu.make_async_remote_copy(
            src_ref=source,
            dst_ref=target,
            send_sem=out_sem,
            recv_sem=in_sem,
            device_id=device(a, b),
            device_id_type=MESH,
        )
        copy.start()
        return copy

    loads = []
    for at, (source, target) in enumerate(
        [
            (cell_hbm, cell_ref),
            (weight_hbm, weight_ref),
            (charge_hbm, charge_ref),
            (fine_hbm, fine_ref),
            (coarse_hbm, coarse_ref),
        ]
    ):
        load = pltpu.make_async_copy(source, target, load_sem.at[at])
        load.start()
        loads.append(load)

    barrier = pltpu.get_barrier_semaphore()
    for a, b in AROUND:
        pl.semaphore_signal(barrier, inc=1, device_id=device(a, b), device_id_type=MESH)

    for load in loads:
        load.wait()

    far_total[...] = jnp.zeros_like(far_total)
    near_total[...] = jnp.zeros_like(near_total)

    def block_at(step, size):
        start = pl.multiple_of(step * size, size)
        return pl.ds(start, size), iota((1, size), 1) + start < live

    def add_rows(sums, parts, depth):
        high, low = split(jnp.concatenate(parts, axis=0))
        both = lax.dot_general(
            jnp.concatenate([high, low], axis=0), depth, LANES_BOTH, preferred_element_type=F32
        )
        sums[...] += both[: high.shape[0]] + both[high.shape[0] :]

    def spread_far(step, carry):
        here, alive = block_at(step, FAR_BLOCK)
        weights = weight_ref[:, here].astype(F32)
        rows_first, rows_second, depth = bead_tables(cell_ref[:, here], weights)
        all_first[:, here] = rows_first
        all_second[:, here] = rows_second
        all_depth[:, here] = depth
        rows_first = rows_first * jnp.where(alive, charge_ref[:, here], 0.0)
        parts = [rows_first[x : x + 1] * rows_second[:16] for x in range(16, 19)]
        parts += [rows_second[y : y + 1] * rows_first for y in range(16, 19)]
        parts += [jnp.zeros((8, FAR_BLOCK), F32)]
        add_rows(far_total, parts, depth)
        return carry

    def spread_near(step, carry):
        here, alive = block_at(step, NEAR_BLOCK)
        rows_first = all_first[0:16, here] * jnp.where(alive, charge_ref[:, here], 0.0)
        rows_second = all_second[0:16, here]
        parts = [rows_first[x : x + 1] * rows_second for x in range(16)]
        add_rows(near_total, parts, all_depth[:, here])
        return carry

    slots = charge_ref.shape[1]
    lax.fori_loop(0, slots // FAR_BLOCK, spread_far, 0)
    main_far[...] = far_total[0:48].reshape(3, 16, LZ)
    tail[...] = far_total[48:120].reshape(3, 24, LZ)

    pl.semaphore_wait(barrier, 8)

    spills_first = [
        send(main_far, side_first, send_1.at[0], recv_1.at[0], 1, 0),
        send(tail.at[:, 16:24], side_both, send_1.at[1], recv_1.at[1], 1, 1),
    ]
    spills_second = [
        send(tail, side_second, send_1.at[2], recv_1.at[2], 0, 1),
        send(main_far.at[:, 8:16], beside.at[0], send_1.at[3], recv_1.at[3], 0, 1),
        send(main_far.at[:, 0:8], beside.at[1], send_1.at[4], recv_1.at[4], 0, -1),
    ]

    lax.fori_loop(0, slots // NEAR_BLOCK, spread_near, 0)

    for copy in spills_second:
        copy.wait()
    charges[...] = near_total[...].reshape(16, 16, LZ)
    beyond[:, 0:8] = beside[0]
    beyond[:, 8:24] = main_far[...]
    beyond[:, 24:32] = beside[1]
    for y in range(3):
        charges[:, y, :] += side_second[y, 0:16]
        beyond[:, 8 + y, :] += side_second[y, 16:19]
        beyond[:, 24 + y, :] += tail[y, 16:19]
    grid[8:24, 8:24] = charges[...].astype(BF16).astype(F32)

    out_edge[0, 3:8] = grid[11:16, 8:24].astype(BF16)
    out_edge[1] = grid[16:24, 8:24].astype(BF16)
    for i in range(2):
        for j in range(2):
            quarter = grid[8 + 8 * i : 16 + 8 * i, 8 + 8 * j : 16 + 8 * j]
            out_corner[2 * i + j] = quarter.reshape(4, 16, LZ).astype(BF16)
    halos = []
    for at, (source, target, a, b) in enumerate(
        [
            (charges.at[0:3], low_edge, -1, 0),
            (out_edge.at[1], in_edge.at[1], 1, 0),
            (out_edge.at[0, 3:8], in_edge.at[0, 3:8], -1, 0),
            (charges.at[0:3, 0:8], low_corner.at[0], -1, -1),
            (charges.at[0:3, 8:16], low_corner.at[1], -1, 1),
            (out_corner.at[2], in_corner.at[2], 1, -1),
            (out_corner.at[3], in_corner.at[3], 1, 1),
            (out_corner.at[0, 1:4], in_corner.at[0, 1:4], -1, -1),
            (out_corner.at[1, 1:4], in_corner.at[1, 1:4], -1, 1),
        ]
    ):
        halos.append(send(source, target, send_2.at[at], recv_2.at[at], a, b))

    lanes = iota((SIDE, LZ), 1)
    taps = iota((SIDE, LZ), 0)
    for at, source in enumerate((fine_ref, coarse_ref)):
        whole = [jnp.zeros((SIDE, LZ), F32)] * 2
        for chunk in range(5):
            placed = jnp.zeros((SIDE, LZ), F32)
            for j in range(4):
                dx = 4 * chunk + j
                if dx < SIDE:
                    place = (lanes == taps + 32 * j).astype(BF16)
                    placed = placed + lax.dot_general(
                        source[dx], place, ROWS_BOTH, preferred_element_type=F32
                    )
            whole.append(placed)
        whole = jnp.concatenate(whole + [jnp.zeros((SIDE, LZ), F32)], axis=1)
        for v in range(4):
            moved = whole if v == 0 else pltpu.roll(whole, STRIP - 32 * v, 1)
            for chunk in range(1, 7):
                lines[at, v, chunk, 0:SIDE] = moved[:, 128 * chunk : 128 * chunk + 128]

    for strips in (fine_strips, coarse_strips):
        strips[:, :, :, 0:128] = jnp.zeros((SIDE, 4, 16, 128), BF16)
        strips[:, :, :, 896:1024] = jnp.zeros((SIDE, 4, 16, 128), BF16)
        strips[:, 0, :, 128:256] = jnp.zeros((SIDE, 16, 128), BF16)
        strips[:, 1:4, :, 768:896] = jnp.zeros((SIDE, 3, 16, 128), BF16)

    def build(dz, carry):
        for at, strips in enumerate((fine_strips, coarse_strips)):
            for v in range(4):
                for chunk in range(2, 7) if v == 0 else range(1, 6):
                    span = slice(128 * chunk, 128 * chunk + 128)
                    line = lines[at, v, chunk, pl.ds(dz, 1)]
                    upper = pltpu.roll(
                        jnp.broadcast_to(line, (8, LZ)), 0, 1, stride=1, stride_axis=0
                    )
                    both = jnp.concatenate([upper, pltpu.roll(upper, 8, 1)], axis=0)
                    strips[dz, v, :, span] = both.astype(BF16)
        return carry

    lax.fori_loop(0, SIDE, build, 0)
    wide_coarse[...] = jnp.zeros_like(wide_coarse)

    for copy in spills_first:
        copy.wait()
    for y in range(3):
        side_first[:, y, :] += side_both[y, 0:3]
    grid[8:11, 8:24] = (charges[0:3] + side_first[...]).astype(BF16).astype(F32)
    out_edge[2] = grid[8:24, 8:16].reshape(8, 16, LZ).astype(BF16)
    out_edge[3] = grid[8:24, 16:24].reshape(8, 16, LZ).astype(BF16)
    for at, b in ((2, -1), (3, 1)):
        halos.append(
            send(out_edge.at[at], in_edge.at[at], send_2.at[7 + at], recv_2.at[7 + at], 0, b)
        )
    for copy in halos:
        copy.wait()
    grid[27:32, 8:24] = in_edge[0, 3:8].astype(F32)
    grid[24:27, 8:24] = (low_edge[...] + beyond[:, 8:24]).astype(BF16).astype(F32)
    grid[24:27, 24:32] = (low_corner[0] + beyond[:, 24:32]).astype(BF16).astype(F32)
    grid[24:27, 0:8] = (low_corner[1] + beyond[:, 0:8]).astype(BF16).astype(F32)
    grid[0:8, 8:24] = in_edge[1].astype(F32)
    grid[8:24, 24:32] = in_edge[2].astype(F32).reshape(16, 8, LZ)
    grid[8:24, 0:8] = in_edge[3].astype(F32).reshape(16, 8, LZ)
    for j in range(2):
        y = 24 - 24 * j
        upper_quarter = in_corner[j, 1:4].astype(F32).reshape(6, 8, LZ)
        grid[27:32, y : y + 8] = upper_quarter[1:6]
        grid[0:8, y : y + 8] = in_corner[2 + j].astype(F32).reshape(8, 8, LZ)

    gap = (iota((LZ, LZ), 0) - 2 * (iota((LZ, LZ), 1) & 63) + 2) & 127
    spline = jnp.where(gap == 2, 0.75, 0.0)
    spline = jnp.where((gap == 1) | (gap == 3), 0.5, spline)
    spline = jnp.where((gap == 0) | (gap == 4), 0.125, spline).astype(BF16)
    coarse_lines = jnp.dot(
        grid[4:27].reshape(23 * 32, LZ).astype(BF16), spline, preferred_element_type=F32
    ).reshape(23, 32, LZ)
    for i in range(10):
        summed[i] = (
            0.125 * (coarse_lines[2 * i] + coarse_lines[2 * i + 4])
            + 0.5 * (coarse_lines[2 * i + 1] + coarse_lines[2 * i + 3])
            + 0.75 * coarse_lines[2 * i + 2]
        )
    for i in range(10):
        parts = [summed[i, pl.ds(4 + t, 10, stride=2)] for t in range(5)]
        plane = 0.125 * (parts[0] + parts[4]) + 0.5 * (parts[1] + parts[3]) + 0.75 * parts[2]
        own_coarse[i, 0:10] = plane.astype(BF16).astype(F32)
    lower = iota((8, LZ), 1) < 64
    inner = [own_coarse[1 + i, 1:9] for i in range(8)]
    pairs = [jnp.where(lower, inner[2 * j], inner[2 * j + 1]) for j in range(4)]
    mains = [jnp.concatenate(pairs[2 * k : 2 * k + 2], axis=0).astype(BF16) for k in range(2)]
    columns = {1: own_coarse[1:9, 0, :], -1: own_coarse[1:9, 9, :], 0: inner[0]}
    coarse_sends = []
    for at, (a, b) in enumerate(AROUND):
        x = 0 if a > 0 else 9
        y = 0 if b > 0 else 9
        outer = jnp.where(lower, own_coarse[x, 1:9], columns[b])
        corner = jnp.broadcast_to(own_coarse[x, y : y + 1], (8, LZ))
        out_coarse[at, 0] = mains[0]
        out_coarse[at, 1] = mains[1]
        out_coarse[at, 2] = jnp.concatenate([outer, corner], axis=0).astype(BF16)
        coarse_sends.append(
            send(out_coarse.at[at], in_coarse.at[at], send_3.at[at], recv_3.at[at], a, b)
        )
    for i in range(8):
        wide_coarse[9 + i, 9:17] = inner[i]

    def strip_rows(strips, dz):
        columns = []
        for q in range(3):
            blocks = []
            for x in range(8):
                a, v = divmod(8 - x + 8 * q, 4)
                blocks.append(strips[dz, v, :, 128 * a : 128 * a + 256])
            columns.append(jnp.concatenate(blocks, axis=0))
        return jnp.concatenate(columns, axis=1)

    operand[:, 0:LZ] = grid[0:24].reshape(768, LZ).astype(BF16)
    operand[:, LZ:] = grid[8:32].reshape(768, LZ).astype(BF16)
    total[...] = jnp.zeros_like(total)

    def products(strips, right, group):
        rows = jnp.concatenate([strip_rows(strips, dz) for dz in group], axis=0)
        result = jnp.dot(rows, right, preferred_element_type=F32)
        return [result[128 * at : 128 * at + 128] for at in range(len(group))]

    def turned(value, dz):
        return value if dz == 8 else pltpu.roll(value, (136 - dz) % 128, 1)

    def correlate_fine(first, last):
        for start in range(first, last, GROUP):
            group = range(start, min(start + GROUP, last))
            for dz, product in zip(group, products(fine_strips, operand[...], group)):
                total[0] += turned(product[:, :LZ], dz)
                total[1] += turned(product[:, LZ:], dz)

    correlate_fine(0, SIDE)

    for at in (6, 7, 0, 1, 2, 3, 4, 5):
        copy = coarse_sends[at]
        copy.wait()
        a, b = AROUND[at]
        x, y = 9 - 8 * a, 9 - 8 * b
        for k in range(2):
            pair_rows = in_coarse[at, k].astype(F32)
            for j in range(2):
                pair = pair_rows[8 * j : 8 * j + 8]
                other = pltpu.roll(pair, 64, 1)
                place = x + 4 * k + 2 * j
                wide_coarse[place, y : y + 8] = jnp.where(lower, pair, other)
                wide_coarse[place + 1, y : y + 8] = jnp.where(lower, other, pair)
        outer_rows = in_coarse[at, 2].astype(F32)
        outer = outer_rows[0:8]
        other = pltpu.roll(outer, 64, 1)
        x_outer = 0 if a > 0 else 25
        y_outer = 0 if b > 0 else 25
        if a != 0:
            wide_coarse[x_outer, y : y + 8] = jnp.where(lower, outer, other)
        if b != 0:
            wide_coarse[x : x + 8, y_outer, :] = jnp.where(lower, other, outer)
        if a != 0 and b != 0:
            wide_coarse[x_outer, y_outer : y_outer + 1] = outer_rows[8:9]
    operand[:, 0:LZ] = wide_coarse[0:24].reshape(768, LZ).astype(BF16)
    operand[:, LZ:] = wide_coarse[8:32].reshape(768, LZ).astype(BF16)
    wide_pot[...] = jnp.zeros_like(wide_pot)

    for start in range(0, SIDE, GROUP):
        group = range(start, min(start + GROUP, SIDE))
        for dz, product in zip(group, products(coarse_strips, operand[...], group)):
            wide_pot[0:8] += turned(product[:, :LZ], dz).reshape(8, 16, LZ)
            wide_pot[8:10] += turned(product[0:32, LZ:], dz).reshape(2, 16, LZ)

    for i in range(8):
        rows_pot[2 * i] = (wide_pot[i] + 6.0 * wide_pot[i + 1] + wide_pot[i + 2]) * 0.125
        rows_pot[2 * i + 1] = (wide_pot[i + 1] + wide_pot[i + 2]) * 0.5
    below = rows_pot[:, 0:8]
    middle = rows_pot[:, 1:9]
    above = rows_pot[:, 2:10]
    even_rows = (below + 6.0 * middle + above) * 0.125
    odd_rows = (middle + above) * 0.5
    for i in range(16):
        potential[i, pl.ds(0, 8, stride=2)] = even_rows[i]
        potential[i, pl.ds(1, 8, stride=2)] = odd_rows[i]
    source = iota((LZ, LZ), 0)
    offset = (iota((LZ, LZ), 1) - 2 * source + 2) & 127
    refine = jnp.where(offset == 2, 0.75, 0.0)
    refine = jnp.where((offset == 1) | (offset == 3), 0.5, refine)
    refine = jnp.where((offset == 0) | (offset == 4), 0.125, refine)
    refine = jnp.where(source < 64, refine, 0.0).astype(BF16)
    high, low = split(potential[...].reshape(256, LZ))
    smooth = jnp.dot(
        jnp.concatenate([high, low], axis=1),
        jnp.concatenate([refine, refine], axis=0),
        preferred_element_type=F32,
    )
    potential[...] = (total[...].reshape(256, LZ) + smooth).reshape(16, 16, LZ)

    for y in range(3):
        send_tail[y] = potential[:, y, :]
    upper = [
        send(potential.at[0:3], upper_first, send_5.at[0], recv_5.at[0], -1, 0),
        send(send_tail.at[:, 0:8], upper_both, send_5.at[2], recv_5.at[2], -1, -1),
        send(send_tail, upper_second, send_5.at[1], recv_5.at[1], 0, -1),
    ]
    grid_ref[...] = potential[...]

    def put_table(start, rows):
        high, low = split(rows)
        read_table[start : start + rows.shape[0], 0:LZ] = high
        read_table[start : start + rows.shape[0], LZ:] = low

    put_table(0, potential[...].reshape(256, LZ))

    def read_near(step, carry):
        here, _ = block_at(step, READ_BLOCK)
        depth = all_depth[:, here]
        along = jnp.dot(
            read_table[0:256], jnp.concatenate([depth, depth], axis=0), preferred_element_type=F32
        )
        rows_first = all_first[:, here]
        near = jnp.zeros((16, READ_BLOCK), F32)
        for x in range(16):
            near = near + rows_first[x : x + 1] * along[16 * x : 16 * x + 16]
        near = near * all_second[0:16, here]
        bead_ref[:, here] = jnp.sum(near[:8] + near[8:], axis=0, keepdims=True)
        return carry

    lax.fori_loop(0, slots // READ_BLOCK, read_near, 0)

    for copy in upper:
        copy.wait()
    put_table(256, upper_first[...].reshape(48, LZ))
    ends = []
    for y in range(3):
        ends += [upper_second[y], upper_both[y]]
    ends += [jnp.zeros((8, LZ), F32)]
    put_table(304, jnp.concatenate(ends, axis=0))

    def read_far(step, carry):
        here, alive = block_at(step, READ_BLOCK)
        depth = all_depth[:, here]
        along = jnp.dot(
            read_table[256:384],
            jnp.concatenate([depth, depth], axis=0),
            preferred_element_type=F32,
        )
        rows_first = all_first[:, here]
        rows_second = all_second[:, here]
        near = jnp.zeros((16, READ_BLOCK), F32)
        for x in range(3):
            near = near + rows_first[16 + x : 17 + x] * along[16 * x : 16 * x + 16]
        far = jnp.zeros((24, READ_BLOCK), F32)
        for y in range(3):
            far = far + rows_second[16 + y : 17 + y] * along[48 + 24 * y : 72 + 24 * y]
        near = near * rows_second[:16]
        far = far * rows_first
        both = near[:8] + near[8:] + far[:8] + far[8:16] + far[16:]
        value = bead_ref[:, here] + jnp.sum(both, axis=0, keepdims=True)
        bead_ref[:, here] = jnp.where(alive, value, 0.0)
        return carry

    lax.fori_loop(0, slots // READ_BLOCK, read_far, 0)


def hand_over(bead_from, grid_from, bead_to, grid_to):
    bead_to[...] = bead_from[...]
    grid_to[...] = grid_from[...]


def on_device(sizes, bead_charge, bead_cell, bead_count, interp_weights, kernel_fine, kernel_coarse):
    slots = bead_charge.shape[-1]
    charge = bead_charge.reshape(1, slots)
    cells = bead_cell.reshape(1, slots)
    weights = interp_weights.reshape(12, slots)
    vmem = pl.BlockSpec(memory_space=pltpu.VMEM)
    smem = pl.BlockSpec(memory_space=pltpu.SMEM)
    anywhere = pl.BlockSpec(memory_space=pl.ANY)
    dma = pltpu.SemaphoreType.DMA
    scratch = [
        pltpu.VMEM((1, slots), F32),
        pltpu.VMEM((1, slots), jnp.int32),
        pltpu.VMEM((12, slots), BF16),
        pltpu.VMEM((SIDE, SIDE, SIDE), BF16),
        pltpu.VMEM((SIDE, SIDE, SIDE), BF16),
        dma((5,)),
        pltpu.VMEM((24, slots), F32),
        pltpu.VMEM((24, slots), F32),
        pltpu.VMEM((LZ, slots), BF16),
        pltpu.VMEM((128, LZ), F32),
        pltpu.VMEM((256, LZ), F32),
        pltpu.VMEM((3, 16, LZ), F32),
        pltpu.VMEM((3, 24, LZ), F32),
        pltpu.VMEM((3, 16, LZ), F32),
        pltpu.VMEM((3, 24, LZ), F32),
        pltpu.VMEM((3, 8, LZ), F32),
        pltpu.VMEM((2, 3, 8, LZ), F32),
        pltpu.VMEM((3, 32, LZ), F32),
        pltpu.VMEM((3, 16, LZ), F32),
        pltpu.VMEM((2, 3, 8, LZ), F32),
        pltpu.VMEM((16, 16, LZ), F32),
        pltpu.VMEM((4, 8, 16, LZ), BF16),
        pltpu.VMEM((4, 4, 16, LZ), BF16),
        pltpu.VMEM((4, 8, 16, LZ), BF16),
        pltpu.VMEM((4, 4, 16, LZ), BF16),
        pltpu.VMEM((32, 32, LZ), F32),
        pltpu.VMEM((768, 2 * LZ), BF16),
        pltpu.VMEM((10, 32, LZ), F32),
        pltpu.VMEM((2, 4, 8, 24, LZ), F32),
        pltpu.VMEM((SIDE, 4, 16, STRIP), BF16),
        pltpu.VMEM((SIDE, 4, 16, STRIP), BF16),
        pltpu.VMEM((10, 16, LZ), F32),
        pltpu.VMEM((8, 3, 16, LZ), BF16),
        pltpu.VMEM((8, 3, 16, LZ), BF16),
        pltpu.VMEM((32, 32, LZ), F32),
        pltpu.VMEM((2, LZ, LZ), F32),
        pltpu.VMEM((10, 16, LZ), F32),
        pltpu.VMEM((16, 16, LZ), F32),
        pltpu.VMEM((3, 16, LZ), F32),
        pltpu.VMEM((16, 16, LZ), F32),
        pltpu.VMEM((3, 16, LZ), F32),
        pltpu.VMEM((3, 16, LZ), F32),
        pltpu.VMEM((3, 8, LZ), F32),
        pltpu.VMEM((ROWS, 2 * LZ), BF16),
    ]
    for count in (5, 11, 8, 3):
        scratch += [dma((count,)), dma((count,))]
    bead, grid = pl.pallas_call(
        functools.partial(melt_kernel, sizes),
        out_shape=(
            jax.ShapeDtypeStruct((1, slots), F32),
            jax.ShapeDtypeStruct((16, 16, LZ), F32),
        ),
        in_specs=[smem] + [anywhere] * 5,
        out_specs=(vmem, vmem),
        scratch_shapes=scratch,
        compiler_params=pltpu.CompilerParams(
            collective_id=0, has_side_effects=True, vmem_limit_bytes=60 << 20
        ),
        name="melt",
    )(bead_count, charge, cells, weights, kernel_fine, kernel_coarse)
    bead, grid = pl.pallas_call(
        hand_over,
        out_shape=(
            jax.ShapeDtypeStruct((1, slots), F32),
            jax.ShapeDtypeStruct((16, 16, LZ), F32),
        ),
        in_specs=[vmem, vmem],
        out_specs=(vmem, vmem),
        name="hand_over",
    )(bead, grid)
    return (bead.reshape(1, 1, slots), grid)


def solution(mesh):
    sizes = (mesh.shape["gx"], mesh.shape["gy"])
    return jax.shard_map(
        functools.partial(on_device, sizes),
        mesh=mesh,
        in_specs=(
            P("gx", "gy", None),
            P("gx", "gy", None),
            P("gx", "gy"),
            P("gx", "gy", None, None),
            P(),
            P(),
        ),
        out_specs=(P("gx", "gy", None), P("gx", "gy", None)),
        check_vma=False,
    )
```

```python
import functools

import jax
import jax.numpy as jnp
from jax import lax
from jax.experimental import pallas as pl
from jax.experimental.pallas import tpu as pltpu
from jax.sharding import PartitionSpec as P

LX = 16
LY = 16
LZ = 128
SIDE = 17
FAR_BLOCK = 8192
NEAR_BLOCK = 8192
READ_BLOCK = 16384
ROWS = 384
STRIP = 1024
GROUP = 5
MESH = pl.DeviceIdType.MESH
F32 = jnp.float32
BF16 = jnp.bfloat16
LANES_BOTH = (((1,), (1,)), ((), ()))
ROWS_BOTH = (((0,), (0,)), ((), ()))
AROUND = [(a, b) for a in (-1, 1, 0) for b in (0, -1, 1) if (a, b) != (0, 0)]


def iota(shape, dim):
    return lax.broadcasted_iota(jnp.int32, shape, dim)


def split(value):
    high = value.astype(BF16)
    low = (value - high.astype(F32)).astype(BF16)
    return high, low


def bead_tables(cells, weights):
    count = cells.shape[1]
    first = cells >> 11
    second = (cells >> 7) & 15
    third = cells & 127
    rows = iota((24, count), 0)
    away_first = rows - first
    away_second = rows - second
    rows_first = jnp.zeros((24, count), F32)
    rows_second = jnp.zeros((24, count), F32)
    for tap in range(4):
        rows_first = jnp.where(away_first == tap, weights[tap : tap + 1], rows_first)
        rows_second = jnp.where(away_second == tap, weights[4 + tap : 5 + tap], rows_second)
    depth = jnp.zeros((LZ, count), BF16)
    places = iota((LZ, count), 0).astype(F32).astype(BF16)
    for tap in range(4):
        target = ((third + tap) & 127).astype(F32).astype(BF16)
        depth = jnp.where(places == target, weights[8 + tap : 9 + tap].astype(BF16), depth)
    return rows_first, rows_second, depth


def melt_kernel(
    sizes,
    count_ref,
    charge_hbm,
    cell_hbm,
    weight_hbm,
    fine_hbm,
    coarse_hbm,
    bead_ref,
    grid_ref,
    charge_ref,
    cell_ref,
    weight_ref,
    fine_ref,
    coarse_ref,
    load_sem,
    all_first,
    all_second,
    all_depth,
    far_total,
    near_total,
    main_far,
    tail,
    side_first,
    side_second,
    side_both,
    beside,
    beyond,
    low_edge,
    low_corner,
    charges,
    out_edge,
    out_corner,
    in_edge,
    in_corner,
    grid,
    operand,
    summed,
    lines,
    fine_strips,
    coarse_strips,
    own_coarse,
    out_coarse,
    in_coarse,
    wide_coarse,
    total,
    wide_pot,
    rows_pot,
    send_tail,
    potential,
    upper_first,
    upper_second,
    upper_both,
    read_table,
    send_1,
    recv_1,
    send_2,
    recv_2,
    send_3,
    recv_3,
    send_5,
    recv_5,
):
    here_first = lax.axis_index("gx")
    here_second = lax.axis_index("gy")
    live = count_ref[0, 0]

    def device(a, b):
        return (
            lax.rem(here_first + (a + sizes[0]), sizes[0]),
            lax.rem(here_second + (b + sizes[1]), sizes[1]),
        )

    def send(source, target, out_sem, in_sem, a, b):
        copy = pltpu.make_async_remote_copy(
            src_ref=source,
            dst_ref=target,
            send_sem=out_sem,
            recv_sem=in_sem,
            device_id=device(a, b),
            device_id_type=MESH,
        )
        copy.start()
        return copy

    loads = []
    for at, (source, target) in enumerate(
        [
            (cell_hbm, cell_ref),
            (weight_hbm, weight_ref),
            (charge_hbm, charge_ref),
            (fine_hbm, fine_ref),
            (coarse_hbm, coarse_ref),
        ]
    ):
        load = pltpu.make_async_copy(source, target, load_sem.at[at])
        load.start()
        loads.append(load)

    barrier = pltpu.get_barrier_semaphore()
    for a, b in AROUND:
        pl.semaphore_signal(barrier, inc=1, device_id=device(a, b), device_id_type=MESH)

    for load in loads:
        load.wait()

    far_total[...] = jnp.zeros_like(far_total)
    near_total[...] = jnp.zeros_like(near_total)

    def block_at(step, size):
        start = pl.multiple_of(step * size, size)
        return pl.ds(start, size), iota((1, size), 1) + start < live

    def add_rows(sums, parts, depth):
        high, low = split(jnp.concatenate(parts, axis=0))
        both = lax.dot_general(
            jnp.concatenate([high, low], axis=0), depth, LANES_BOTH, preferred_element_type=F32
        )
        sums[...] += both[: high.shape[0]] + both[high.shape[0] :]

    def spread_far(step, carry):
        here, alive = block_at(step, FAR_BLOCK)
        weights = weight_ref[:, here].astype(F32)
        rows_first, rows_second, depth = bead_tables(cell_ref[:, here], weights)
        all_first[:, here] = rows_first
        all_second[:, here] = rows_second
        all_depth[:, here] = depth
        rows_first = rows_first * jnp.where(alive, charge_ref[:, here], 0.0)
        parts = [rows_first[x : x + 1] * rows_second[:16] for x in range(16, 19)]
        parts += [rows_second[y : y + 1] * rows_first for y in range(16, 19)]
        parts += [jnp.zeros((8, FAR_BLOCK), F32)]
        add_rows(far_total, parts, depth)
        return carry

    def spread_near(step, carry):
        here, alive = block_at(step, NEAR_BLOCK)
        rows_first = all_first[0:16, here] * jnp.where(alive, charge_ref[:, here], 0.0)
        rows_second = all_second[0:16, here]
        parts = [rows_first[x : x + 1] * rows_second for x in range(16)]
        add_rows(near_total, parts, all_depth[:, here])
        return carry

    slots = charge_ref.shape[1]
    lax.fori_loop(0, slots // FAR_BLOCK, spread_far, 0)
    main_far[...] = far_total[0:48].reshape(3, 16, LZ)
    tail[...] = far_total[48:120].reshape(3, 24, LZ)

    pl.semaphore_wait(barrier, 8)

    spills_first = [
        send(main_far, side_first, send_1.at[0], recv_1.at[0], 1, 0),
        send(tail.at[:, 16:24], side_both, send_1.at[1], recv_1.at[1], 1, 1),
    ]
    spills_second = [
        send(tail, side_second, send_1.at[2], recv_1.at[2], 0, 1),
        send(main_far.at[:, 8:16], beside.at[0], send_1.at[3], recv_1.at[3], 0, 1),
        send(main_far.at[:, 0:8], beside.at[1], send_1.at[4], recv_1.at[4], 0, -1),
    ]

    lax.fori_loop(0, slots // NEAR_BLOCK, spread_near, 0)

    for copy in spills_second:
        copy.wait()
    charges[...] = near_total[...].reshape(16, 16, LZ)
    beyond[:, 0:8] = beside[0]
    beyond[:, 8:24] = main_far[...]
    beyond[:, 24:32] = beside[1]
    for y in range(3):
        charges[:, y, :] += side_second[y, 0:16]
        beyond[:, 8 + y, :] += side_second[y, 16:19]
        beyond[:, 24 + y, :] += tail[y, 16:19]
    grid[8:24, 8:24] = charges[...].astype(BF16).astype(F32)

    out_edge[0, 3:8] = grid[11:16, 8:24].astype(BF16)
    out_edge[1] = grid[16:24, 8:24].astype(BF16)
    for i in range(2):
        for j in range(2):
            quarter = grid[8 + 8 * i : 16 + 8 * i, 8 + 8 * j : 16 + 8 * j]
            out_corner[2 * i + j] = quarter.reshape(4, 16, LZ).astype(BF16)
    halos = []
    for at, (source, target, a, b) in enumerate(
        [
            (charges.at[0:3], low_edge, -1, 0),
            (out_edge.at[1], in_edge.at[1], 1, 0),
            (out_edge.at[0, 3:8], in_edge.at[0, 3:8], -1, 0),
            (charges.at[0:3, 0:8], low_corner.at[0], -1, -1),
            (charges.at[0:3, 8:16], low_corner.at[1], -1, 1),
            (out_corner.at[2], in_corner.at[2], 1, -1),
            (out_corner.at[3], in_corner.at[3], 1, 1),
            (out_corner.at[0, 1:4], in_corner.at[0, 1:4], -1, -1),
            (out_corner.at[1, 1:4], in_corner.at[1, 1:4], -1, 1),
        ]
    ):
        halos.append(send(source, target, send_2.at[at], recv_2.at[at], a, b))

    lanes = iota((SIDE, LZ), 1)
    taps = iota((SIDE, LZ), 0)
    for at, source in enumerate((fine_ref, coarse_ref)):
        whole = [jnp.zeros((SIDE, LZ), F32)] * 2
        for chunk in range(5):
            placed = jnp.zeros((SIDE, LZ), F32)
            for j in range(4):
                dx = 4 * chunk + j
                if dx < SIDE:
                    place = (lanes == taps + 32 * j).astype(BF16)
                    placed = placed + lax.dot_general(
                        source[dx], place, ROWS_BOTH, preferred_element_type=F32
                    )
            whole.append(placed)
        whole = jnp.concatenate(whole + [jnp.zeros((SIDE, LZ), F32)], axis=1)
        for v in range(4):
            moved = whole if v == 0 else pltpu.roll(whole, STRIP - 32 * v, 1)
            for chunk in range(1, 7):
                lines[at, v, chunk, 0:SIDE] = moved[:, 128 * chunk : 128 * chunk + 128]

    for strips in (fine_strips, coarse_strips):
        strips[:, :, :, 0:128] = jnp.zeros((SIDE, 4, 16, 128), BF16)
        strips[:, :, :, 896:1024] = jnp.zeros((SIDE, 4, 16, 128), BF16)
        strips[:, 0, :, 128:256] = jnp.zeros((SIDE, 16, 128), BF16)
        strips[:, 1:4, :, 768:896] = jnp.zeros((SIDE, 3, 16, 128), BF16)

    def build(dz, carry):
        for at, strips in enumerate((fine_strips, coarse_strips)):
            for v in range(4):
                for chunk in range(2, 7) if v == 0 else range(1, 6):
                    span = slice(128 * chunk, 128 * chunk + 128)
                    line = lines[at, v, chunk, pl.ds(dz, 1)]
                    upper = pltpu.roll(
                        jnp.broadcast_to(line, (8, LZ)), 0, 1, stride=1, stride_axis=0
                    )
                    both = jnp.concatenate([upper, pltpu.roll(upper, 8, 1)], axis=0)
                    strips[dz, v, :, span] = both.astype(BF16)
        return carry

    lax.fori_loop(0, SIDE, build, 0)
    wide_coarse[...] = jnp.zeros_like(wide_coarse)

    for copy in spills_first:
        copy.wait()
    for y in range(3):
        side_first[:, y, :] += side_both[y, 0:3]
    grid[8:11, 8:24] = (charges[0:3] + side_first[...]).astype(BF16).astype(F32)
    out_edge[2] = grid[8:24, 8:16].reshape(8, 16, LZ).astype(BF16)
    out_edge[3] = grid[8:24, 16:24].reshape(8, 16, LZ).astype(BF16)
    for at, b in ((2, -1), (3, 1)):
        halos.append(
            send(out_edge.at[at], in_edge.at[at], send_2.at[7 + at], recv_2.at[7 + at], 0, b)
        )
    for copy in halos:
        copy.wait()
    grid[27:32, 8:24] = in_edge[0, 3:8].astype(F32)
    grid[24:27, 8:24] = (low_edge[...] + beyond[:, 8:24]).astype(BF16).astype(F32)
    grid[24:27, 24:32] = (low_corner[0] + beyond[:, 24:32]).astype(BF16).astype(F32)
    grid[24:27, 0:8] = (low_corner[1] + beyond[:, 0:8]).astype(BF16).astype(F32)
    grid[0:8, 8:24] = in_edge[1].astype(F32)
    grid[8:24, 24:32] = in_edge[2].astype(F32).reshape(16, 8, LZ)
    grid[8:24, 0:8] = in_edge[3].astype(F32).reshape(16, 8, LZ)
    for j in range(2):
        y = 24 - 24 * j
        upper_quarter = in_corner[j, 1:4].astype(F32).reshape(6, 8, LZ)
        grid[27:32, y : y + 8] = upper_quarter[1:6]
        grid[0:8, y : y + 8] = in_corner[2 + j].astype(F32).reshape(8, 8, LZ)

    gap = (iota((LZ, LZ), 0) - 2 * (iota((LZ, LZ), 1) & 63) + 2) & 127
    spline = jnp.where(gap == 2, 0.75, 0.0)
    spline = jnp.where((gap == 1) | (gap == 3), 0.5, spline)
    spline = jnp.where((gap == 0) | (gap == 4), 0.125, spline).astype(BF16)
    coarse_lines = jnp.dot(
        grid[4:27].reshape(23 * 32, LZ).astype(BF16), spline, preferred_element_type=F32
    ).reshape(23, 32, LZ)
    for i in range(10):
        summed[i] = (
            0.125 * (coarse_lines[2 * i] + coarse_lines[2 * i + 4])
            + 0.5 * (coarse_lines[2 * i + 1] + coarse_lines[2 * i + 3])
            + 0.75 * coarse_lines[2 * i + 2]
        )
    for i in range(10):
        parts = [summed[i, pl.ds(4 + t, 10, stride=2)] for t in range(5)]
        plane = 0.125 * (parts[0] + parts[4]) + 0.5 * (parts[1] + parts[3]) + 0.75 * parts[2]
        own_coarse[i, 0:10] = plane.astype(BF16).astype(F32)
    lower = iota((8, LZ), 1) < 64
    inner = [own_coarse[1 + i, 1:9] for i in range(8)]
    pairs = [jnp.where(lower, inner[2 * j], inner[2 * j + 1]) for j in range(4)]
    mains = [jnp.concatenate(pairs[2 * k : 2 * k + 2], axis=0).astype(BF16) for k in range(2)]
    columns = {1: own_coarse[1:9, 0, :], -1: own_coarse[1:9, 9, :], 0: inner[0]}
    coarse_sends = []
    for at, (a, b) in enumerate(AROUND):
        x = 0 if a > 0 else 9
        y = 0 if b > 0 else 9
        outer = jnp.where(lower, own_coarse[x, 1:9], columns[b])
        corner = jnp.broadcast_to(own_coarse[x, y : y + 1], (8, LZ))
        out_coarse[at, 0] = mains[0]
        out_coarse[at, 1] = mains[1]
        out_coarse[at, 2] = jnp.concatenate([outer, corner], axis=0).astype(BF16)
        coarse_sends.append(
            send(out_coarse.at[at], in_coarse.at[at], send_3.at[at], recv_3.at[at], a, b)
        )
    for i in range(8):
        wide_coarse[9 + i, 9:17] = inner[i]

    def strip_rows(strips, dz):
        columns = []
        for q in range(3):
            blocks = []
            for x in range(8):
                a, v = divmod(8 - x + 8 * q, 4)
                blocks.append(strips[dz, v, :, 128 * a : 128 * a + 256])
            columns.append(jnp.concatenate(blocks, axis=0))
        return jnp.concatenate(columns, axis=1)

    operand[:, 0:LZ] = grid[0:24].reshape(768, LZ).astype(BF16)
    operand[:, LZ:] = grid[8:32].reshape(768, LZ).astype(BF16)
    total[...] = jnp.zeros_like(total)

    def products(strips, right, group):
        rows = jnp.concatenate([strip_rows(strips, dz) for dz in group], axis=0)
        result = jnp.dot(rows, right, preferred_element_type=F32)
        return [result[128 * at : 128 * at + 128] for at in range(len(group))]

    def turned(value, dz):
        return value if dz == 8 else pltpu.roll(value, (136 - dz) % 128, 1)

    def correlate_fine(first, last):
        for start in range(first, last, GROUP):
            group = range(start, min(start + GROUP, last))
            for dz, product in zip(group, products(fine_strips, operand[...], group)):
                total[0] += turned(product[:, :LZ], dz)
                total[1] += turned(product[:, LZ:], dz)

    correlate_fine(0, SIDE)

    for at in (6, 7, 0, 1, 2, 3, 4, 5):
        copy = coarse_sends[at]
        copy.wait()
        a, b = AROUND[at]
        x, y = 9 - 8 * a, 9 - 8 * b
        for k in range(2):
            pair_rows = in_coarse[at, k].astype(F32)
            for j in range(2):
                pair = pair_rows[8 * j : 8 * j + 8]
                other = pltpu.roll(pair, 64, 1)
                place = x + 4 * k + 2 * j
                wide_coarse[place, y : y + 8] = jnp.where(lower, pair, other)
                wide_coarse[place + 1, y : y + 8] = jnp.where(lower, other, pair)
        outer_rows = in_coarse[at, 2].astype(F32)
        outer = outer_rows[0:8]
        other = pltpu.roll(outer, 64, 1)
        x_outer = 0 if a > 0 else 25
        y_outer = 0 if b > 0 else 25
        if a != 0:
            wide_coarse[x_outer, y : y + 8] = jnp.where(lower, outer, other)
        if b != 0:
            wide_coarse[x : x + 8, y_outer, :] = jnp.where(lower, other, outer)
        if a != 0 and b != 0:
            wide_coarse[x_outer, y_outer : y_outer + 1] = outer_rows[8:9]
    operand[:, 0:LZ] = wide_coarse[0:24].reshape(768, LZ).astype(BF16)
    operand[:, LZ:] = wide_coarse[8:32].reshape(768, LZ).astype(BF16)
    wide_pot[...] = jnp.zeros_like(wide_pot)

    for start in range(0, SIDE, GROUP):
        group = range(start, min(start + GROUP, SIDE))
        for dz, product in zip(group, products(coarse_strips, operand[...], group)):
            wide_pot[0:8] += turned(product[:, :LZ], dz).reshape(8, 16, LZ)
            wide_pot[8:10] += turned(product[0:32, LZ:], dz).reshape(2, 16, LZ)

    for i in range(8):
        rows_pot[2 * i] = (wide_pot[i] + 6.0 * wide_pot[i + 1] + wide_pot[i + 2]) * 0.125
        rows_pot[2 * i + 1] = (wide_pot[i + 1] + wide_pot[i + 2]) * 0.5
    below = rows_pot[:, 0:8]
    middle = rows_pot[:, 1:9]
    above = rows_pot[:, 2:10]
    even_rows = (below + 6.0 * middle + above) * 0.125
    odd_rows = (middle + above) * 0.5
    for i in range(16):
        potential[i, pl.ds(0, 8, stride=2)] = even_rows[i]
        potential[i, pl.ds(1, 8, stride=2)] = odd_rows[i]
    source = iota((LZ, LZ), 0)
    offset = (iota((LZ, LZ), 1) - 2 * source + 2) & 127
    refine = jnp.where(offset == 2, 0.75, 0.0)
    refine = jnp.where((offset == 1) | (offset == 3), 0.5, refine)
    refine = jnp.where((offset == 0) | (offset == 4), 0.125, refine)
    refine = jnp.where(source < 64, refine, 0.0).astype(BF16)
    high, low = split(potential[...].reshape(256, LZ))
    smooth = jnp.dot(
        jnp.concatenate([high, low], axis=1),
        jnp.concatenate([refine, refine], axis=0),
        preferred_element_type=F32,
    )
    potential[...] = (total[...].reshape(256, LZ) + smooth).reshape(16, 16, LZ)

    for y in range(3):
        send_tail[y] = potential[:, y, :]
    upper = [
        send(potential.at[0:3], upper_first, send_5.at[0], recv_5.at[0], -1, 0),
        send(send_tail.at[:, 0:8], upper_both, send_5.at[2], recv_5.at[2], -1, -1),
        send(send_tail, upper_second, send_5.at[1], recv_5.at[1], 0, -1),
    ]
    grid_ref[...] = potential[...]

    def put_table(start, rows):
        high, low = split(rows)
        read_table[start : start + rows.shape[0], 0:LZ] = high
        read_table[start : start + rows.shape[0], LZ:] = low

    put_table(0, potential[...].reshape(256, LZ))

    def read_near(step, carry):
        here, _ = block_at(step, READ_BLOCK)
        depth = all_depth[:, here]
        along = jnp.dot(
            read_table[0:256], jnp.concatenate([depth, depth], axis=0), preferred_element_type=F32
        )
        rows_first = all_first[:, here]
        near = jnp.zeros((16, READ_BLOCK), F32)
        for x in range(16):
            near = near + rows_first[x : x + 1] * along[16 * x : 16 * x + 16]
        near = near * all_second[0:16, here]
        bead_ref[:, here] = jnp.sum(near[:8] + near[8:], axis=0, keepdims=True)
        return carry

    lax.fori_loop(0, slots // READ_BLOCK, read_near, 0)

    for copy in upper:
        copy.wait()
    put_table(256, upper_first[...].reshape(48, LZ))
    ends = []
    for y in range(3):
        ends += [upper_second[y], upper_both[y]]
    ends += [jnp.zeros((8, LZ), F32)]
    put_table(304, jnp.concatenate(ends, axis=0))

    def read_far(step, carry):
        here, alive = block_at(step, READ_BLOCK)
        depth = all_depth[:, here]
        along = jnp.dot(
            read_table[256:384],
            jnp.concatenate([depth, depth], axis=0),
            preferred_element_type=F32,
        )
        rows_first = all_first[:, here]
        rows_second = all_second[:, here]
        near = jnp.zeros((16, READ_BLOCK), F32)
        for x in range(3):
            near = near + rows_first[16 + x : 17 + x] * along[16 * x : 16 * x + 16]
        far = jnp.zeros((24, READ_BLOCK), F32)
        for y in range(3):
            far = far + rows_second[16 + y : 17 + y] * along[48 + 24 * y : 72 + 24 * y]
        near = near * rows_second[:16]
        far = far * rows_first
        both = near[:8] + near[8:] + far[:8] + far[8:16] + far[16:]
        value = bead_ref[:, here] + jnp.sum(both, axis=0, keepdims=True)
        bead_ref[:, here] = jnp.where(alive, value, 0.0)
        return carry

    lax.fori_loop(0, slots // READ_BLOCK, read_far, 0)


def hand_over(bead_from, grid_from, bead_to, grid_to):
    bead_to[...] = bead_from[...]
    grid_to[...] = grid_from[...]


def on_device(sizes, bead_charge, bead_cell, bead_count, interp_weights, kernel_fine, kernel_coarse):
    slots = bead_charge.shape[-1]
    charge = bead_charge.reshape(1, slots)
    cells = bead_cell.reshape(1, slots)
    weights = interp_weights.reshape(12, slots)
    vmem = pl.BlockSpec(memory_space=pltpu.VMEM)
    smem = pl.BlockSpec(memory_space=pltpu.SMEM)
    anywhere = pl.BlockSpec(memory_space=pl.ANY)
    dma = pltpu.SemaphoreType.DMA
    scratch = [
        pltpu.VMEM((1, slots), F32),
        pltpu.VMEM((1, slots), jnp.int32),
        pltpu.VMEM((12, slots), BF16),
        pltpu.VMEM((SIDE, SIDE, SIDE), BF16),
        pltpu.VMEM((SIDE, SIDE, SIDE), BF16),
        dma((5,)),
        pltpu.VMEM((24, slots), F32),
        pltpu.VMEM((24, slots), F32),
        pltpu.VMEM((LZ, slots), BF16),
        pltpu.VMEM((128, LZ), F32),
        pltpu.VMEM((256, LZ), F32),
        pltpu.VMEM((3, 16, LZ), F32),
        pltpu.VMEM((3, 24, LZ), F32),
        pltpu.VMEM((3, 16, LZ), F32),
        pltpu.VMEM((3, 24, LZ), F32),
        pltpu.VMEM((3, 8, LZ), F32),
        pltpu.VMEM((2, 3, 8, LZ), F32),
        pltpu.VMEM((3, 32, LZ), F32),
        pltpu.VMEM((3, 16, LZ), F32),
        pltpu.VMEM((2, 3, 8, LZ), F32),
        pltpu.VMEM((16, 16, LZ), F32),
        pltpu.VMEM((4, 8, 16, LZ), BF16),
        pltpu.VMEM((4, 4, 16, LZ), BF16),
        pltpu.VMEM((4, 8, 16, LZ), BF16),
        pltpu.VMEM((4, 4, 16, LZ), BF16),
        pltpu.VMEM((32, 32, LZ), F32),
        pltpu.VMEM((768, 2 * LZ), BF16),
        pltpu.VMEM((10, 32, LZ), F32),
        pltpu.VMEM((2, 4, 8, 24, LZ), F32),
        pltpu.VMEM((SIDE, 4, 16, STRIP), BF16),
        pltpu.VMEM((SIDE, 4, 16, STRIP), BF16),
        pltpu.VMEM((10, 16, LZ), F32),
        pltpu.VMEM((8, 3, 16, LZ), BF16),
        pltpu.VMEM((8, 3, 16, LZ), BF16),
        pltpu.VMEM((32, 32, LZ), F32),
        pltpu.VMEM((2, LZ, LZ), F32),
        pltpu.VMEM((10, 16, LZ), F32),
        pltpu.VMEM((16, 16, LZ), F32),
        pltpu.VMEM((3, 16, LZ), F32),
        pltpu.VMEM((16, 16, LZ), F32),
        pltpu.VMEM((3, 16, LZ), F32),
        pltpu.VMEM((3, 16, LZ), F32),
        pltpu.VMEM((3, 8, LZ), F32),
        pltpu.VMEM((ROWS, 2 * LZ), BF16),
    ]
    for count in (5, 11, 8, 3):
        scratch += [dma((count,)), dma((count,))]
    bead, grid = pl.pallas_call(
        functools.partial(melt_kernel, sizes),
        out_shape=(
            jax.ShapeDtypeStruct((1, slots), F32),
            jax.ShapeDtypeStruct((16, 16, LZ), F32),
        ),
        in_specs=[smem] + [anywhere] * 5,
        out_specs=(vmem, vmem),
        scratch_shapes=scratch,
        compiler_params=pltpu.CompilerParams(
            collective_id=0, has_side_effects=True, vmem_limit_bytes=60 << 20
        ),
        name="melt",
    )(bead_count, charge, cells, weights, kernel_fine, kernel_coarse)
    bead, grid = pl.pallas_call(
        hand_over,
        out_shape=(
            jax.ShapeDtypeStruct((1, slots), F32),
            jax.ShapeDtypeStruct((16, 16, LZ), F32),
        ),
        in_specs=[vmem, vmem],
        out_specs=(vmem, vmem),
        name="hand_over",
    )(bead, grid)
    return (bead.reshape(1, 1, slots), grid)


def solution(mesh):
    sizes = (mesh.shape["gx"], mesh.shape["gy"])
    return jax.shard_map(
        functools.partial(on_device, sizes),
        mesh=mesh,
        in_specs=(
            P("gx", "gy", None),
            P("gx", "gy", None),
            P("gx", "gy"),
            P("gx", "gy", None, None),
            P(),
            P(),
        ),
        out_specs=(P("gx", "gy", None), P("gx", "gy", None)),
        check_vma=False,
    )
```
